32 devices in a mesh: dp: 2 (over core), expert: 16 (over z, y, x).
Axes of the slice: x: 2, y: 2, z: 4, core: 2. Of those that a mesh axis runs over, the one named last changes fastest.
Arguments:
- tokens: bfloat16 [4096, 2048], P(('dp', 'expert')), may hold values from -6 to 6
- gates: float32 [4096, 8], P(('dp', 'expert')), may hold values from 0.05 to 0.5
- expert_ids: int32 [4096, 8], P(('dp', 'expert')), may hold values from 0 to 15, as said below
- slots: int32 [4096, 8], P(('dp', 'expert')), may hold values from -1 to 63, as said below
- grad_out: bfloat16 [4096, 2048], P(('dp', 'expert')), may hold values from -6 to 6
- expert_weights: bfloat16 [16, 3, 2048, 768], P('expert', None, None, 'dp'), may hold values from -0.125 to 0.125
Outputs:
- combined: bfloat16 [4096, 2048], P(('dp', 'expert'))
- gate_grads: float32 [4096, 8], P(('dp', 'expert'))
- token_grads: bfloat16 [4096, 2048], P(('dp', 'expert'))
- weight_grads: bfloat16 [16, 3, 2048, 768], P('expert', None, None, 'dp')
The draws below stay inside these ranges and needn't reach their ends.
Inputs may be any that keep to these rules, and one draw needn't show every extreme that they name: `expert_ids`: each token names 8 distinct experts. Within each device block of 128 tokens, the choices are counted in token then choice order for each expert; slots holds that count, or -1 once 64 earlier choices of the block went to that expert.
All inputs are finite; a program needn't handle non-finite values.
Results may differ from the reference program's by a relative error of at most 0.008.
Values may be sent and summed in bfloat16 or wider, within the bound.
No kernel may reach another device: no remote copies, remote signals or barrier semaphores. Data moves between devices by JAX's collectives and lax.ppermute only.
A program may use at most 192 MiB of HBM per device.

```python
import jax
import jax.numpy as jnp
from jax import lax

D = 2048
HID = 768
TOP = 8
TOK_DEV = 128
EXPERTS = 16
CAP = 64
TOKENS = 4096
N_DP = 2


def route_pair(key):
    blocks = TOKENS // TOK_DEV
    starting_offset = jax.random.randint(jax.random.fold_in(key, 11), (TOKENS, EXPERTS), 0, 2 ** 14) * EXPERTS
    column_entry = jnp.arange(EXPERTS, dtype=jnp.int32)[None, :]
    starting_offset = starting_offset + column_entry
    shared_onehot_mask = jax.random.randint(jax.random.fold_in(key, 12), (), 0, EXPERTS)
    block_hot = jax.random.randint(jax.random.fold_in(key, 13), (blocks,), 0, EXPERTS)
    coins = jax.random.randint(jax.random.fold_in(key, 14), (TOKENS, 2), 0, 2)
    orders = jax.vmap(lambda sub: jax.random.permutation(sub, TOK_DEV))(jax.random.split(jax.random.fold_in(key, 15), blocks))
    leading_choice = (orders.reshape(-1) < TOK_DEV // 2) | (coins[:, 0] == 1)
    trailing_choice = coins[:, 1] == 1
    owning_block = jnp.repeat(block_hot, TOK_DEV)
    extra_score = jnp.where(leading_choice[:, None] & (column_entry == shared_onehot_mask), 2 ** 21, 0)
    extra_score = extra_score + jnp.where(trailing_choice[:, None] & (column_entry == owning_block[:, None]), 2 ** 21, 0)
    router_scores = (starting_offset + extra_score).astype(jnp.int32)
    unused, chosen = lax.top_k(router_scores, TOP)
    chosen = chosen.astype(jnp.int32)
    onehot = (chosen.reshape(blocks, TOK_DEV * TOP)[:, :, None] == column_entry[None, :, :]).astype(jnp.int32)
    place = jnp.sum(jnp.cumsum(onehot, axis=1) * onehot, axis=2) - 1
    slot_values = jnp.where(place < CAP, place, -1).reshape(TOKENS, TOP).astype(jnp.int32)
    return (chosen, slot_values)


def draw_expert_ids(key, part):
    return route_pair(key)[0]


def draw_slots(key, part):
    return route_pair(key)[1]


def steps_of(key, extent, pieces, least, top_value):
    factor_of = 1.0
    for dim, parts in pieces:
        draws = jax.random.uniform(jax.random.fold_in(jax.random.fold_in(key, 6), dim), (parts,), jnp.float32, least / len(pieces), top_value / len(pieces))
        factor_of = factor_of * jnp.repeat(jnp.exp(draws), extent[dim] // parts).reshape((-1,) + (1,) * (len(extent) - 1 - dim))
    return factor_of


def scatter_about(own_key, dims, scale, bound, cuts=(), kind=jnp.bfloat16):
    drawn = jax.random.normal(own_key, dims, jnp.float32) * scale
    if len(cuts) > 0:
        drawn = steps_of(own_key, dims, cuts, -0.22, 0.18) * drawn
    return jnp.clip(drawn, min=-bound, max=bound).astype(kind)


def setup_inputs(seed: int = 0) -> dict:
    key_of = jax.random.split(jax.random.key(seed), 7)
    return {
        "tokens": scatter_about(key_of[0], (TOKENS, D), 1.0, 6.0, ((0, 32),)),
        "gates": jnp.clip(0.05 + 0.45 * jax.random.uniform(key_of[1], (TOKENS, TOP), jnp.float32) ** steps_of(key_of[1], (TOKENS, TOP), ((0, 32),), -0.2, 0.2), 0.05, 0.5),
        "expert_ids": draw_expert_ids(jax.random.fold_in(key_of[6], 71), 0),
        "slots": draw_slots(jax.random.fold_in(key_of[6], 71), 0),
        "grad_out": scatter_about(key_of[4], (TOKENS, D), 1.0, 6.0, ((0, 32),)),
        "expert_weights": scatter_about(key_of[5], (EXPERTS, 3, D, HID), D ** -0.5, 0.125, ((0, 16), (3, 2))),
    }


def contract_rows(left, right):
    return lax.dot_general(left, right, (((0,), (0,)), ((), ())), preferred_element_type=jnp.float32)


def contract_last(left, right):
    return lax.dot_general(left, right, (((1,), (1,)), ((), ())), preferred_element_type=jnp.float32)


def expert_pass(inputs, grad_rows, weights):
    gate_pre = jnp.dot(inputs, weights[0], preferred_element_type=jnp.float32)
    up_pre = jnp.dot(inputs, weights[1], preferred_element_type=jnp.float32)
    sigmoid_gate = jax.nn.sigmoid(gate_pre)
    activated = (gate_pre * sigmoid_gate * up_pre).astype(jnp.bfloat16)
    expert_out = contract_last(activated, weights[2]).astype(jnp.bfloat16)
    grad_act = jnp.dot(grad_rows, weights[2], preferred_element_type=jnp.float32)
    grad_gate = (grad_act * up_pre * sigmoid_gate * (1.0 + gate_pre * (1.0 - sigmoid_gate))).astype(jnp.bfloat16)
    grad_up = (grad_act * gate_pre * sigmoid_gate).astype(jnp.bfloat16)
    row_grads = (contract_last(grad_gate, weights[0]) + contract_last(grad_up, weights[1])).astype(jnp.bfloat16)
    stacked = jnp.stack([contract_rows(inputs, grad_gate), contract_rows(inputs, grad_up), contract_rows(grad_rows, activated)])
    return expert_out, row_grads, stacked.astype(jnp.bfloat16)


def reference(tokens, gates, expert_ids, slots, grad_out, expert_weights):
    slot_rows = EXPERTS * CAP
    whole = N_DP * EXPERTS * slot_rows
    position = jnp.arange(TOKENS, dtype=jnp.int32)
    replica = position // (TOK_DEV * EXPERTS)
    source = (position // TOK_DEV) % EXPERTS
    target = jnp.where(slots >= 0, ((expert_ids * N_DP + replica[:, None]) * EXPERTS + source[:, None]) * CAP + slots, whole).astype(jnp.int32)
    anchor = jnp.broadcast_to(position[:, None], (TOKENS, TOP)).astype(jnp.int32)
    holder = jnp.full((whole,), TOKENS, jnp.int32).at[target.reshape(-1)].set(anchor.reshape(-1), mode="drop")
    holder = holder.reshape(EXPERTS, N_DP * slot_rows)
    slot_gate = jnp.zeros((whole,), jnp.float32).at[target.reshape(-1)].set(gates.reshape(-1), mode="drop")
    slot_gate = slot_gate.reshape(EXPERTS, N_DP * slot_rows)
    padding = jnp.zeros((1, D), jnp.bfloat16)
    token_table = jnp.concatenate([tokens, padding], 0)
    grad_table = jnp.concatenate([grad_out, padding], 0)

    def per_expert(index):
        chosen = holder[index]
        inputs = token_table[chosen]
        grad_rows = (slot_gate[index][:, None] * grad_table[chosen].astype(jnp.float32)).astype(jnp.bfloat16)
        return expert_pass(inputs, grad_rows, expert_weights[index])

    expert_out, row_grads, weight_grads = lax.map(per_expert, jnp.arange(EXPERTS, dtype=jnp.int32))
    out_table = jnp.concatenate([expert_out.reshape(-1, D), padding], 0)
    back_table = jnp.concatenate([row_grads.reshape(-1, D), padding], 0)
    combined = jnp.zeros((TOKENS, D), jnp.float32)
    token_grads = jnp.zeros((TOKENS, D), jnp.float32)
    gate_cols = []
    for choice_index in range(TOP):
        picked = out_table[target[:, choice_index]].astype(jnp.float32)
        combined = combined + gates[:, choice_index:choice_index + 1] * picked
        gate_cols.append(jnp.sum(grad_out.astype(jnp.float32) * picked, axis=1))
        token_grads = token_grads + back_table[target[:, choice_index]].astype(jnp.float32)
    gate_grads = jnp.stack(gate_cols, axis=1)
    return combined.astype(jnp.bfloat16), gate_grads, token_grads.astype(jnp.bfloat16), weight_grads
```

```python
import functools

import jax
import jax.numpy as jnp
from jax import lax
from jax.experimental import pallas as pl
from jax.experimental.pallas import tpu as pltpu
from jax.sharding import PartitionSpec as P

F32 = jnp.float32
BF16 = jnp.bfloat16
MIB = 1 << 20
CHUNKS = 4
HBM = pl.BlockSpec(memory_space=pl.ANY)
WHOLE = pl.BlockSpec(memory_space=pltpu.VMEM)
SCALAR = pl.BlockSpec(memory_space=pltpu.SMEM)


def mask_of(table, expert, capacity):
    top = table.shape[0] // 2
    tokens = table.shape[1]
    wanted = (expert * capacity + lax.broadcasted_iota(jnp.int32, (capacity, tokens), 0)).astype(F32)
    hit = jnp.zeros((capacity, tokens), F32)
    for k in range(top):
        hit = hit + jnp.where(table[k : k + 1] == wanted, 1.0, 0.0)
    return hit


def gate_column(table, expert, capacity):
    top = table.shape[0] // 2
    tokens = table.shape[1]
    wanted = (expert * capacity + lax.broadcasted_iota(jnp.int32, (capacity, tokens), 0)).astype(F32)
    gate = jnp.zeros((capacity, tokens), F32)
    for k in range(top):
        gate = gate + jnp.where(table[k : k + 1] == wanted, table[top + k : top + k + 1], 0.0)
    return jnp.sum(gate, axis=1, keepdims=True)


def pick_kernel(capacity, n_half, blocks, me_ref, *refs):
    tables = refs[:n_half]
    arrays = refs[n_half : 3 * n_half]
    own_t, own_g, sent_t, sent_g = refs[3 * n_half :]
    me = me_ref[0]
    for expert, outs in ((me ^ 1, (sent_t, sent_g)), (me, (own_t, own_g))):
        for half in range(n_half):
            for b in range(blocks):
                mask = mask_of(tables[half][b], expert, capacity).astype(BF16)
                tokens = mask.shape[1]
                row = (half * blocks + b) * capacity
                for a in range(2):
                    source = arrays[2 * half + a][b * tokens : (b + 1) * tokens, :]
                    outs[a][row : row + capacity, :] = jnp.dot(
                        mask, source, preferred_element_type=F32
                    ).astype(BF16)


def pick(me, capacity, halves):
    n_half = len(halves)
    blocks = halves[0][0].shape[0]
    width = halves[0][1].shape[1]
    tile = 512
    rows = n_half * blocks * capacity
    in_rows = halves[0][1].shape[0]
    table_spec = pl.BlockSpec(halves[0][0].shape, lambda i: (0, 0, 0))
    in_spec = pl.BlockSpec((in_rows, tile), lambda i: (0, i))
    out_spec = pl.BlockSpec((rows, tile), lambda i: (0, i))
    return pl.pallas_call(
        functools.partial(pick_kernel, capacity, n_half, blocks),
        grid=(width // tile,),
        in_specs=[SCALAR] + [table_spec] * n_half + [in_spec] * (2 * n_half),
        out_specs=[out_spec] * 4,
        out_shape=[jax.ShapeDtypeStruct((rows, width), BF16)] * 4,
        compiler_params=pltpu.CompilerParams(vmem_limit_bytes=24 * MIB),
        cost_estimate=pl.CostEstimate(
            flops=8 * rows * in_rows * width // blocks // n_half,
            bytes_accessed=4 * (n_half * in_rows + 2 * rows) * width,
            transcendentals=0,
        ),
        name="pick",
    )(me, *[h[0] for h in halves], *[a for h in halves for a in h[1:]])


def expert_kernel(capacity, n_piece, blocks, me_ref, tables, w_own, w_other, *refs):
    x_refs = refs[:n_piece]
    g_refs = refs[n_piece : 2 * n_piece]
    (out_own, out_sent, back_own, back_sent, gate_rows, act_ref, dgate_ref, dup_ref) = refs[
        2 * n_piece : 2 * n_piece + 8
    ]
    w, x, g, sem = refs[2 * n_piece + 8 :]
    half = w_own.shape[2]
    hidden = 2 * half
    rows, width = x.shape
    copies = []
    for i in (0, 1, 2):
        pair = []
        for j, source in enumerate((w_own, w_other)):
            copy = pltpu.make_async_copy(
                source.at[i], w.at[i, :, pl.ds(j * half, half)], sem.at[i, j]
            )
            copy.start()
            pair.append(copy)
        copies.append(pair)
    row = 0
    for xr, gr in zip(x_refs, g_refs):
        count = xr.shape[0]
        x[row : row + count, :] = xr[...]
        g[row : row + count, :] = gr[...]
        row += count
    me = me_ref[0]
    groups = tables.shape[0]
    gates = jnp.concatenate(
        [gate_column(tables[i], me, capacity) for i in range(groups)], axis=0
    )
    for pair in copies:
        for copy in pair:
            copy.wait()
    step = 256

    def hidden_tile(n, total):
        cols = pl.ds(pl.multiple_of(n * step, step), step)
        gate_pre = jnp.dot(x[...], w[0, :, cols], preferred_element_type=F32)
        up_pre = jnp.dot(x[...], w[1, :, cols], preferred_element_type=F32)
        pulled = jnp.dot(g[...], w[2, :, cols], preferred_element_type=F32)
        sig = jax.nn.sigmoid(gate_pre)
        silu = gate_pre * sig
        act = silu * up_pre
        grad_act = pulled * gates
        act_ref[:, cols] = (act * gates).astype(BF16)
        dgate_ref[:, cols] = (grad_act * up_pre * sig * (1.0 + gate_pre * (1.0 - sig))).astype(BF16)
        dup_ref[:, cols] = (grad_act * silu).astype(BF16)
        return total + jnp.sum(act * pulled, axis=1, keepdims=True)

    total = lax.fori_loop(0, hidden // step, hidden_tile, jnp.zeros((rows, 1), F32))
    for i in range(groups):
        mask = mask_of(tables[i], me, capacity)
        gate_rows[i : i + 1, :] = jnp.sum(
            mask * total[i * capacity : (i + 1) * capacity], axis=0, keepdims=True
        )
    side = rows // 2
    nt = (((1,), (1,)), ((), ()))

    def width_tile(n, carry):
        cols = pl.ds(pl.multiple_of(n * step, step), step)
        out = lax.dot_general(act_ref[...], w[2, cols, :], nt, preferred_element_type=F32)
        out = out.astype(BF16)
        out_own[:, cols] = out[:side]
        out_sent[:, cols] = out[side:]
        back = lax.dot_general(dgate_ref[...], w[0, cols, :], nt, preferred_element_type=F32)
        back += lax.dot_general(dup_ref[...], w[1, cols, :], nt, preferred_element_type=F32)
        back = back.astype(BF16)
        back_own[:, cols] = back[:side]
        back_sent[:, cols] = back[side:]
        return carry

    lax.fori_loop(0, width // step, width_tile, 0)


def expert(me, capacity, tables, w_own, w_other, x_pieces, g_pieces):
    n_piece = len(x_pieces)
    rows = sum(p.shape[0] for p in x_pieces)
    width = x_pieces[0].shape[1]
    hidden = 2 * w_own.shape[2]
    groups, _, tokens = tables.shape
    return pl.pallas_call(
        functools.partial(expert_kernel, capacity, n_piece, groups),
        in_specs=[SCALAR, WHOLE, HBM, HBM] + [WHOLE] * (2 * n_piece),
        out_specs=[WHOLE] * 8,
        out_shape=[jax.ShapeDtypeStruct((rows // 2, width), BF16)] * 4
        + [jax.ShapeDtypeStruct((groups, tokens), F32)]
        + [jax.ShapeDtypeStruct((rows, hidden), BF16)] * 3,
        scratch_shapes=[
            pltpu.VMEM((3, width, hidden), BF16),
            pltpu.VMEM((rows, width), BF16),
            pltpu.VMEM((rows, width), BF16),
            pltpu.SemaphoreType.DMA((3, 2)),
        ],
        compiler_params=pltpu.CompilerParams(vmem_limit_bytes=44 * MIB),
        cost_estimate=pl.CostEstimate(
            flops=12 * rows * width * hidden,
            bytes_accessed=6 * width * hidden + 8 * rows * width,
            transcendentals=rows * hidden,
        ),
        name="expert",
    )(me, tables, w_own, w_other, *x_pieces, *g_pieces)


def spread(table, me, capacity, own, received):
    mask = jnp.concatenate(
        [mask_of(table, me, capacity), mask_of(table, me ^ 1, capacity)], axis=0
    )
    rows = jnp.concatenate([own, received], axis=0)
    return jnp.dot(mask.T.astype(BF16), rows, preferred_element_type=F32)


def partial_kernel(capacity, blocks, me_ref, tables, own, received, out):
    tokens = tables.shape[2]
    for b in range(blocks):
        rows = pl.ds(b * capacity, capacity)
        out[b * tokens : (b + 1) * tokens, :] = spread(
            tables[b], me_ref[0], capacity, own[rows, :], received[rows, :]
        ).astype(BF16)


def partial_sum(me, capacity, tables, own, received):
    blocks, _, tokens = tables.shape
    width = own.shape[1]
    tile = 1024
    row_spec = pl.BlockSpec((blocks * capacity, tile), lambda i: (1, i))
    return pl.pallas_call(
        functools.partial(partial_kernel, capacity, blocks),
        grid=(width // tile,),
        in_specs=[SCALAR, pl.BlockSpec(tables.shape, lambda i: (0, 0, 0)), row_spec, row_spec],
        out_specs=pl.BlockSpec((blocks * tokens, tile), lambda i: (0, i)),
        out_shape=jax.ShapeDtypeStruct((blocks * tokens, width), BF16),
        compiler_params=pltpu.CompilerParams(vmem_limit_bytes=24 * MIB),
        cost_estimate=pl.CostEstimate(
            flops=4 * blocks * tokens * capacity * width,
            bytes_accessed=2 * blocks * (tokens + 2 * capacity) * width,
            transcendentals=0,
        ),
        name="partial_sum",
    )(me, tables, own, received)


def block_kernel(capacity, me_ref, table, own, received, *refs):
    out = refs[-1]
    total = spread(table[0], me_ref[0], capacity, own[...], received[...])
    for other in refs[:-1]:
        total = total + other[...].astype(F32)
    out[...] = total.astype(BF16)


def block_sum(me, capacity, table, own, received, b, others):
    tokens = table.shape[2]
    width = own.shape[1]
    tile = 1024
    row_spec = pl.BlockSpec((capacity, tile), lambda i: (b, i))
    return pl.pallas_call(
        functools.partial(block_kernel, capacity),
        grid=(width // tile,),
        in_specs=[SCALAR, pl.BlockSpec(table.shape, lambda i: (0, 0, 0)), row_spec, row_spec]
        + [pl.BlockSpec((tokens, tile), lambda i, at=at: (at, i)) for _, at in others],
        out_specs=pl.BlockSpec((tokens, tile), lambda i: (0, i)),
        out_shape=jax.ShapeDtypeStruct((tokens, width), BF16),
        compiler_params=pltpu.CompilerParams(vmem_limit_bytes=24 * MIB),
        cost_estimate=pl.CostEstimate(
            flops=4 * tokens * capacity * width,
            bytes_accessed=2 * (tokens * (1 + len(others)) + 2 * capacity) * width,
            transcendentals=0,
        ),
        name="block_sum",
    )(me, table, own, received, *[a for a, _ in others])


def weight_kernel(n_piece, n_chunk, n_out, *refs):
    left = jnp.concatenate([r[...] for r in refs[:n_piece]], axis=0)
    rights = refs[n_piece : n_piece + n_out * n_chunk]
    outs = refs[n_piece + n_out * n_chunk :]
    tn = (((0,), (0,)), ((), ()))
    for i in range(n_out):
        right = jnp.concatenate([r[...] for r in rights[i * n_chunk : (i + 1) * n_chunk]], axis=0)
        total = lax.dot_general(left, right, tn, preferred_element_type=F32)
        half = total.shape[1] // 2
        outs[2 * i][...] = total[:, :half]
        outs[2 * i + 1][...] = total[:, half:].astype(BF16)


def weight_sums(pieces, rights):
    width = pieces[0].shape[1]
    hidden = rights[0][0].shape[1]
    rows = sum(p.shape[0] for p in pieces)
    tile = 256
    n_out = len(rights)
    flat = [r for group in rights for r in group]
    return pl.pallas_call(
        functools.partial(weight_kernel, len(pieces), len(rights[0]), n_out),
        grid=(width // tile,),
        in_specs=[pl.BlockSpec((p.shape[0], tile), lambda i: (0, i)) for p in pieces]
        + [pl.BlockSpec(r.shape, lambda i: (0, 0)) for r in flat],
        out_specs=[pl.BlockSpec((tile, hidden // 2), lambda i: (i, 0))] * (2 * n_out),
        out_shape=[
            jax.ShapeDtypeStruct((width, hidden // 2), F32),
            jax.ShapeDtypeStruct((width, hidden // 2), BF16),
        ]
        * n_out,
        compiler_params=pltpu.CompilerParams(vmem_limit_bytes=40 * MIB),
        cost_estimate=pl.CostEstimate(
            flops=2 * rows * width * hidden * n_out,
            bytes_accessed=2 * rows * width + n_out * (2 * rows * hidden + 3 * width * hidden),
            transcendentals=0,
        ),
        name="weight_sums",
    )(*pieces, *flat)


def local(tokens, gates, expert_ids, slots, grad_out, expert_weights):
    n_expert = lax.axis_size("expert")
    n_dp = lax.axis_size("dp")
    tok_count, top_count = expert_ids.shape
    capacity = tok_count * top_count // n_expert
    depth = n_expert // 4
    per_chunk = depth // CHUNKS

    def swap(array, flip):
        return lax.ppermute(array, "expert", [(i, i ^ flip) for i in range(n_expert)])

    def swap_dp(array):
        return lax.ppermute(array, "dp", [(i, n_dp - 1 - i) for i in range(n_dp)])

    index = lax.axis_index("expert").astype(jnp.int32)
    me = index.reshape(1)
    key = jnp.where(slots >= 0, expert_ids * capacity + slots, -1)
    table = jnp.concatenate([key.T.astype(F32), gates.T], axis=0)[None]

    pair = jnp.concatenate([table, swap(table, 2)], axis=0)
    near = [pair] + [swap(pair, 4 * s) for s in range(1, depth)]
    near = jnp.stack(near)
    far = swap(near, 1)

    w_own = expert_weights[0]
    w_other = swap_dp(w_own)

    pair_t = [tokens] + [swap(tokens, 4 * s) for s in range(1, depth)]
    pair_g = [grad_out] + [swap(grad_out, 4 * s) for s in range(1, depth)]

    def chunk_rows(blocks, c):
        part = blocks[c * per_chunk : (c + 1) * per_chunk]
        return part[0] if len(part) == 1 else jnp.concatenate(part, axis=0)

    x_pieces, g_pieces, acts, dgates, dups, gate_rows = [], [], [], [], [], []
    outs, backs = [], []
    for c in range(CHUNKS):
        zs = slice(c * per_chunk, (c + 1) * per_chunk)
        here_t, here_g = chunk_rows(pair_t, c), chunk_rows(pair_g, c)
        there_t, there_g = swap(here_t, 2), swap(here_g, 2)
        first = (near[zs, 0], here_t, here_g)
        second = (near[zs, 1], there_t, there_g)
        picks = [[first], [second]] if c == 0 else [[first, second]]
        own_t, own_g, got_t, got_g = [], [], [], []
        for halves in picks:
            a, b, sent_t, sent_g = pick(me, capacity, halves)
            own_t.append(a)
            own_g.append(b)
            got_t.append(swap(sent_t, 1))
            got_g.append(swap(sent_g, 1))
        tables = jnp.concatenate([near[zs, 0], near[zs, 1], far[zs, 0], far[zs, 1]], axis=0)
        out_own, out_sent, back_own, back_sent, rows, act, dgate, dup = expert(
            me, capacity, tables, w_own, w_other, own_t + got_t, own_g + got_g
        )
        x_pieces += own_t + got_t
        g_pieces += own_g + got_g
        acts.append(act)
        dgates.append(dgate)
        dups.append(dup)
        gate_rows.append(rows.reshape(2, 2, per_chunk, tok_count))
        outs.append((out_own, out_sent))
        backs.append((back_own, back_sent))

    results = []
    for sent in (outs, backs):
        waiting = []
        final = None
        for c in reversed(range(CHUNKS)):
            zs = slice(c * per_chunk, (c + 1) * per_chunk)
            own, given = sent[c]
            received = swap(given, 1)
            from_y = swap(partial_sum(me, capacity, near[zs, 1], own, received), 2)
            for b in reversed(range(per_chunk)):
                s = c * per_chunk + b
                if s > 0:
                    part = block_sum(
                        me, capacity, near[s : s + 1, 0], own, received, b, [(from_y, b)]
                    )
                    waiting.append((swap(part, 4 * s), 0))
                else:
                    final = block_sum(
                        me, capacity, near[0:1, 0], own, received, 0, [(from_y, 0)] + waiting
                    )
        results.append(final)
    combined, token_grads = results

    own0, other0, own1, other1 = weight_sums(x_pieces, [dgates, dups])
    own2, other2 = weight_sums(g_pieces, [acts])
    weight_grads = jnp.stack(
        [
            (own + swap_dp(other).astype(F32)).astype(BF16)
            for own, other in ((own0, other0), (own1, other1), (own2, other2))
        ]
    )[None]

    sums = jnp.stack(gate_rows)
    sums = sums.transpose(1, 2, 0, 3, 4).reshape(2, 2, depth, tok_count)
    sums = jnp.stack([sums[0], swap(sums[1], 1)])
    sums = jnp.stack([sums[:, 0], swap(sums[:, 1], 2)])
    sums = jnp.stack([sums[:, :, 0]] + [swap(sums[:, :, s], 4 * s) for s in range(1, depth)])
    sums = sums.reshape(n_expert, tok_count)
    source = jnp.arange(n_expert, dtype=jnp.int32) ^ index
    hit = (expert_ids[:, :, None] == source[None, None, :]) & (slots >= 0)[:, :, None]
    gate_grads = jnp.sum(jnp.where(hit, sums.T[:, None, :], 0.0), axis=2)
    return (combined, gate_grads, token_grads, weight_grads)


def solution(mesh):
    placed = (
        P(("dp", "expert"), None),
        P(("dp", "expert"), None),
        P(("dp", "expert"), None),
        P(("dp", "expert"), None),
        P(("dp", "expert"), None),
        P("expert", None, None, "dp"),
    )
    return jax.shard_map(
        local,
        mesh=mesh,
        in_specs=placed,
        out_specs=(
            P(("dp", "expert"), None),
            P(("dp", "expert"), None),
            P(("dp", "expert"), None),
            P("expert", None, None, "dp"),
        ),
        check_vma=False,
    )
```

```python
import functools

import jax
import jax.numpy as jnp
from jax import lax
from jax.experimental import pallas as pl
from jax.experimental.pallas import tpu as pltpu
from jax.sharding import PartitionSpec as P

F32 = jnp.float32
BF16 = jnp.bfloat16
MIB = 1 << 20
CHUNKS = 4
HBM = pl.BlockSpec(memory_space=pl.ANY)
WHOLE = pl.BlockSpec(memory_space=pltpu.VMEM)
SCALAR = pl.BlockSpec(memory_space=pltpu.SMEM)


def mask_of(table, expert, capacity):
    top = table.shape[0] // 2
    tokens = table.shape[1]
    wanted = (expert * capacity + lax.broadcasted_iota(jnp.int32, (capacity, tokens), 0)).astype(F32)
    hit = jnp.zeros((capacity, tokens), F32)
    for k in range(top):
        hit = hit + jnp.where(table[k : k + 1] == wanted, 1.0, 0.0)
    return hit


def gate_column(table, expert, capacity):
    top = table.shape[0] // 2
    tokens = table.shape[1]
    wanted = (expert * capacity + lax.broadcasted_iota(jnp.int32, (capacity, tokens), 0)).astype(F32)
    gate = jnp.zeros((capacity, tokens), F32)
    for k in range(top):
        gate = gate + jnp.where(table[k : k + 1] == wanted, table[top + k : top + k + 1], 0.0)
    return jnp.sum(gate, axis=1, keepdims=True)


def pick_kernel(capacity, flip, blocks, n_deps, me_ref, *refs):
    tables, arrays = refs[:2], refs[2:4]
    own, sent = refs[4 + n_deps :]
    me = me_ref[0]
    for expert, out in ((me ^ flip, sent), (me, own)):
        for half in range(2):
            for b in range(blocks):
                mask = mask_of(tables[half][b], expert, capacity).astype(BF16)
                tokens = mask.shape[1]
                row = (half * blocks + b) * capacity
                source = arrays[half][b * tokens : (b + 1) * tokens, :]
                out[row : row + capacity, :] = jnp.dot(
                    mask, source, preferred_element_type=F32
                ).astype(BF16)


def pick(me, flip, capacity, tables, here, there, deps=()):
    blocks = tables[0].shape[0]
    in_rows, width = here.shape
    tile = 1024
    rows = 2 * blocks * capacity
    table_spec = pl.BlockSpec(tables[0].shape, lambda i: (0, 0, 0))
    in_spec = pl.BlockSpec((in_rows, tile), lambda i: (0, i))
    out_spec = pl.BlockSpec((rows, tile), lambda i: (0, i))
    return pl.pallas_call(
        functools.partial(pick_kernel, capacity, flip, blocks, len(deps)),
        grid=(width // tile,),
        in_specs=[SCALAR, table_spec, table_spec, in_spec, in_spec] + [HBM] * len(deps),
        out_specs=[out_spec] * 2,
        out_shape=[jax.ShapeDtypeStruct((rows, width), BF16)] * 2,
        compiler_params=pltpu.CompilerParams(vmem_limit_bytes=24 * MIB),
        cost_estimate=pl.CostEstimate(
            flops=8 * capacity * in_rows * width,
            bytes_accessed=4 * (in_rows + rows) * width,
            transcendentals=0,
        ),
        name="pick",
    )(me, *tables, here, there, *deps)


def expert_kernel(capacity, n_deps, me_ref, tables, weights, *refs):
    own_t, got_t, own_g, got_g = refs[:4]
    (out_own, out_sent, back_own, back_sent, gate_rows, act_out, dgate_out, dup_out) = refs[
        4 + n_deps : 12 + n_deps
    ]
    (w, x, g, gate_up, act_ref, dgate_ref, dup_ref, out, back, row_sem, w_sem, out_sem) = refs[
        12 + n_deps :
    ]
    half = weights.shape[3]
    hidden = 2 * half
    rows, width = x.shape
    side, quarter = rows // 2, rows // 4

    def started(source, target, sem):
        copy = pltpu.make_async_copy(source, target, sem)
        copy.start()
        return copy

    def row_quarters(q):
        return pl.ds(q * quarter, quarter)

    first, second = pl.ds(0, side), pl.ds(side, side)
    x_copies = [
        started(own_t, x.at[first], row_sem.at[0]),
        started(got_t, x.at[second], row_sem.at[1]),
    ]
    w_copies = [
        [started(weights.at[j, i], w.at[i, :, pl.ds(j * half, half)], w_sem.at[i, j]) for j in (0, 1)]
        for i in (0, 1)
    ]
    g_copies = [
        started(own_g.at[row_quarters(0)], g.at[row_quarters(0)], row_sem.at[2]),
        started(got_g.at[row_quarters(0)], g.at[row_quarters(1)], row_sem.at[3]),
        started(own_g.at[row_quarters(1)], g.at[row_quarters(2)], row_sem.at[4]),
        started(got_g.at[row_quarters(1)], g.at[row_quarters(3)], row_sem.at[5]),
    ]
    w_copies.append(
        [started(weights.at[j, 2], w.at[2, :, pl.ds(j * half, half)], w_sem.at[2, j]) for j in (0, 1)]
    )
    me = me_ref[0]
    groups = tables.shape[0]
    gates = jnp.concatenate(
        [gate_column(tables[i], me, capacity) for i in range(groups)], axis=0
    )
    step = 256

    def pre(i):
        def tile(n, carry):
            cols = pl.ds(pl.multiple_of(n * step, step), step)
            gate_up[i, :, cols] = jnp.dot(x[...], w[i, :, cols], preferred_element_type=F32)
            return carry

        lax.fori_loop(0, hidden // step, tile, 0, unroll=True)

    for copy in x_copies + w_copies[0]:
        copy.wait()
    pre(0)
    for copy in w_copies[1]:
        copy.wait()
    pre(1)
    for copy in g_copies + w_copies[2]:
        copy.wait()

    def hidden_tile(n, total):
        cols = pl.ds(pl.multiple_of(n * step, step), step)
        gate_pre, up_pre = gate_up[0, :, cols], gate_up[1, :, cols]
        pulled = jnp.dot(g[...], w[2, :, cols], preferred_element_type=F32)
        sig = jax.nn.sigmoid(gate_pre)
        silu = gate_pre * sig
        act = silu * up_pre
        grad_act = pulled * gates
        act_ref[:, cols] = (act * gates).astype(BF16)
        dgate_ref[:, cols] = (grad_act * up_pre * sig * (1.0 + gate_pre * (1.0 - sig))).astype(BF16)
        dup_ref[:, cols] = (grad_act * silu).astype(BF16)
        return total + jnp.sum(act * pulled, axis=1, keepdims=True)

    total = lax.fori_loop(0, hidden // step, hidden_tile, jnp.zeros((rows, 1), F32), unroll=True)
    copies = [
        started(act_ref, act_out, out_sem.at[0]),
        started(dgate_ref, dgate_out, out_sem.at[1]),
        started(dup_ref, dup_out, out_sem.at[2]),
    ]
    for i in range(groups):
        mask = mask_of(tables[i], me, capacity)
        gate_rows[i : i + 1, :] = jnp.sum(
            mask * total[i * capacity : (i + 1) * capacity], axis=0, keepdims=True
        )
    nt = (((1,), (1,)), ((), ()))

    def out_tile(n, carry):
        cols = pl.ds(pl.multiple_of(n * step, step), step)
        out[:, cols] = lax.dot_general(
            act_ref[...], w[2, cols, :], nt, preferred_element_type=F32
        ).astype(BF16)
        return carry

    def back_tile(n, carry):
        cols = pl.ds(pl.multiple_of(n * step, step), step)
        total = lax.dot_general(dgate_ref[...], w[0, cols, :], nt, preferred_element_type=F32)
        total += lax.dot_general(dup_ref[...], w[1, cols, :], nt, preferred_element_type=F32)
        back[:, cols] = total.astype(BF16)
        return carry

    lax.fori_loop(0, width // step, out_tile, 0, unroll=True)
    copies += [
        started(out.at[first], out_own, out_sem.at[3]),
        started(out.at[second], out_sent, out_sem.at[4]),
    ]
    lax.fori_loop(0, width // step, back_tile, 0, unroll=True)
    copies += [
        started(back.at[row_quarters(0)], back_own.at[row_quarters(0)], out_sem.at[5]),
        started(back.at[row_quarters(1)], back_sent.at[row_quarters(0)], out_sem.at[6]),
        started(back.at[row_quarters(2)], back_own.at[row_quarters(1)], out_sem.at[7]),
        started(back.at[row_quarters(3)], back_sent.at[row_quarters(1)], out_sem.at[8]),
    ]
    for copy in copies:
        copy.wait()


def expert(me, capacity, tables, weights, own_t, got_t, own_g, got_g, deps=()):
    rows, width = 2 * own_t.shape[0], own_t.shape[1]
    hidden = 2 * weights.shape[3]
    groups, _, tokens = tables.shape
    return pl.pallas_call(
        functools.partial(expert_kernel, capacity, len(deps)),
        in_specs=[SCALAR, WHOLE, HBM] + [HBM] * 4 + [HBM] * len(deps),
        out_specs=[HBM] * 4 + [WHOLE] + [HBM] * 3,
        out_shape=[jax.ShapeDtypeStruct((rows // 2, width), BF16)] * 4
        + [jax.ShapeDtypeStruct((groups, tokens), F32)]
        + [jax.ShapeDtypeStruct((rows, hidden), BF16)] * 3,
        scratch_shapes=[
            pltpu.VMEM((3, width, hidden), BF16),
            pltpu.VMEM((rows, width), BF16),
            pltpu.VMEM((rows, width), BF16),
            pltpu.VMEM((2, rows, hidden), F32),
            pltpu.VMEM((rows, hidden), BF16),
            pltpu.VMEM((rows, hidden), BF16),
            pltpu.VMEM((rows, hidden), BF16),
            pltpu.VMEM((rows, width), BF16),
            pltpu.VMEM((rows, width), BF16),
            pltpu.SemaphoreType.DMA((6,)),
            pltpu.SemaphoreType.DMA((3, 2)),
            pltpu.SemaphoreType.DMA((9,)),
        ],
        compiler_params=pltpu.CompilerParams(vmem_limit_bytes=60 * MIB),
        cost_estimate=pl.CostEstimate(
            flops=12 * rows * width * hidden,
            bytes_accessed=24 * width * hidden,
            transcendentals=rows * hidden,
        ),
        name="expert",
    )(me, tables, weights, own_t, got_t, own_g, got_g, *deps)


def sum_kernel(capacity, flip, n_other, n_deps, me_ref, tables, own, received, *refs):
    others, out = refs[:n_other], refs[n_other + n_deps]
    blocks, _, tokens = tables.shape
    me = me_ref[0]
    for b in range(blocks):
        here = slice(b * tokens, (b + 1) * tokens)
        slots = slice(b * capacity, (b + 1) * capacity)
        mask = jnp.concatenate(
            [mask_of(tables[b], me, capacity), mask_of(tables[b], me ^ flip, capacity)], axis=0
        )
        rows = jnp.concatenate([own[slots, :], received[slots, :]], axis=0)
        total = jnp.dot(mask.T.astype(BF16), rows, preferred_element_type=F32)
        for other in others:
            total = total + other[here, :].astype(F32)
        out[here, :] = total.astype(BF16)


def token_sum(me, flip, capacity, tables, own, received, half, others=(), deps=()):
    blocks, _, tokens = tables.shape
    width = own.shape[1]
    tile = 1024
    row_spec = pl.BlockSpec((blocks * capacity, tile), lambda i: (half, i))
    sum_spec = pl.BlockSpec((blocks * tokens, tile), lambda i: (0, i))
    return pl.pallas_call(
        functools.partial(sum_kernel, capacity, flip, len(others), len(deps)),
        grid=(width // tile,),
        in_specs=[SCALAR, pl.BlockSpec(tables.shape, lambda i: (0, 0, 0)), row_spec, row_spec]
        + [sum_spec] * len(others)
        + [HBM] * len(deps),
        out_specs=sum_spec,
        out_shape=jax.ShapeDtypeStruct((blocks * tokens, width), BF16),
        compiler_params=pltpu.CompilerParams(vmem_limit_bytes=24 * MIB),
        cost_estimate=pl.CostEstimate(
            flops=4 * blocks * tokens * capacity * width,
            bytes_accessed=2 * blocks * (tokens * (1 + len(others)) + 2 * capacity) * width,
            transcendentals=0,
        ),
        name="token_sum",
    )(me, tables, own, received, *others, *deps)


def pair_kernel(capacity, n_more, me_ref, tables, *refs):
    mores, outs = refs[6 : 6 + 2 * n_more], refs[6 + 2 * n_more :]
    blocks, _, tokens = tables.shape
    me = me_ref[0]
    for b in range(blocks):
        here = slice(b * tokens, (b + 1) * tokens)
        slots = slice(b * capacity, (b + 1) * capacity)
        mine = mask_of(tables[b], me, capacity)
        for a, flip in ((0, 1), (1, 2)):
            own, got, part = refs[3 * a : 3 * a + 3]
            mask = jnp.concatenate([mine, mask_of(tables[b], me ^ flip, capacity)], axis=0)
            rows = jnp.concatenate([own[slots, :], got[slots, :]], axis=0)
            total = jnp.dot(mask.T.astype(BF16), rows, preferred_element_type=F32)
            total = total + part[here, :].astype(F32)
            for more in mores[a::2]:
                total = total + more[here, :].astype(F32)
            if len(outs) == 1:
                outs[0][a, here, :] = total.astype(BF16)
            else:
                outs[a][here, :] = total.astype(BF16)


def pair_sum(me, capacity, tables, out, back, mores=(), split=False):
    blocks, _, tokens = tables.shape
    width = out[0].shape[1]
    tile = 512
    rows = blocks * tokens
    row_spec = pl.BlockSpec((blocks * capacity, tile), lambda i: (0, i))
    sum_spec = pl.BlockSpec((rows, tile), lambda i: (0, i))
    pair_spec = pl.BlockSpec((2, rows, tile), lambda i: (0, 0, i))
    single = jax.ShapeDtypeStruct((rows, width), BF16)
    half_specs = [pl.BlockSpec((None, rows, tile), lambda i, a=a: (a, 0, i)) for a in range(2)]
    mores = [
        (m, [sum_spec] * 2) if isinstance(m, (list, tuple)) else ((m, m), half_specs) for m in mores
    ]
    result = pl.pallas_call(
        functools.partial(pair_kernel, capacity, len(mores)),
        grid=(width // tile,),
        in_specs=[SCALAR, pl.BlockSpec(tables.shape, lambda i: (0, 0, 0))]
        + [row_spec, row_spec, sum_spec] * 2
        + [s for _, specs in mores for s in specs],
        out_specs=[sum_spec] * 2 if split else pair_spec,
        out_shape=[single] * 2 if split else jax.ShapeDtypeStruct((2, rows, width), BF16),
        compiler_params=pltpu.CompilerParams(vmem_limit_bytes=24 * MIB),
        cost_estimate=pl.CostEstimate(
            flops=8 * rows * capacity * width,
            bytes_accessed=4 * blocks * (tokens * (2 + len(mores)) + 2 * capacity) * width,
            transcendentals=0,
        ),
        name="pair_sum",
    )(me, tables, *out, *back, *[m for pair, _ in mores for m in pair])
    return result


def weight_kernel(n_chunk, n_out, reorder, n_held, me_ref, *refs):
    left = jnp.concatenate([r[...] for r in refs[: 2 * n_chunk]], axis=0)
    rights = refs[2 * n_chunk : (2 + n_out) * n_chunk]
    own, other = refs[(2 + n_out) * n_chunk + n_held :]
    lower = me_ref[1] == 0
    tn = (((0,), (0,)), ((), ()))
    for i in range(n_out):
        parts = []
        for r in rights[i * n_chunk : (i + 1) * n_chunk]:
            quarter = r.shape[0] // 4
            for q in (0, 2, 1, 3) if reorder else range(4):
                parts.append(r[q * quarter : (q + 1) * quarter, :])
        right = jnp.concatenate(parts, axis=0)
        total = lax.dot_general(left, right, tn, preferred_element_type=F32)
        half = total.shape[1] // 2
        own[i] = jnp.where(lower, total[:, :half], total[:, half:])
        other[i] = jnp.where(lower, total[:, half:], total[:, :half]).astype(BF16)


def weight_sums(me, pieces, rights, reorder, at, before=()):
    width = pieces[0].shape[1]
    hidden = rights[0][0].shape[1]
    rows = sum(p.shape[0] for p in pieces)
    tile = 256
    n_out = len(rights)
    flat = [r for group in rights for r in group]
    n_in = 1 + len(pieces) + len(flat)
    return pl.pallas_call(
        functools.partial(weight_kernel, len(rights[0]), n_out, reorder, len(before)),
        grid=(width // tile,),
        in_specs=[SCALAR]
        + [pl.BlockSpec((p.shape[0], tile), lambda i: (0, i)) for p in pieces]
        + [pl.BlockSpec(r.shape, lambda i: (0, 0)) for r in flat]
        + [HBM] * len(before),
        out_specs=[pl.BlockSpec((n_out, tile, hidden // 2), lambda i: (at // n_out, i, 0))] * 2,
        out_shape=[
            jax.ShapeDtypeStruct((3, width, hidden // 2), F32),
            jax.ShapeDtypeStruct((3, width, hidden // 2), BF16),
        ],
        input_output_aliases={n_in + i: i for i in range(len(before))},
        compiler_params=pltpu.CompilerParams(vmem_limit_bytes=60 * MIB),
        cost_estimate=pl.CostEstimate(
            flops=2 * rows * width * hidden * n_out,
            bytes_accessed=n_out * 20 * width * hidden,
            transcendentals=0,
        ),
        name="weight_sums",
    )(me, *pieces, *flat, *before)


class Held(dict):
    def fence(self):
        names = list(self)
        for name, value in zip(names, lax.optimization_barrier([self[n] for n in names])):
            self[name] = value


def after(array, *deps):
    return lax.optimization_barrier((array, *deps))[0]


def local(tokens, gates, expert_ids, slots, grad_out, expert_weights):
    n_expert = lax.axis_size("expert")
    tok_count, top_count = expert_ids.shape
    capacity = tok_count * top_count // n_expert
    depth = n_expert // 4
    many = depth // CHUNKS
    FLIP_X, FLIP_Y, FLIP_NEAR, FLIP_FAR = 1, 2, 4 * many, 8 * many

    def swap(array, flip):
        return lax.ppermute(array, "expert", [(i, i ^ flip) for i in range(n_expert)])

    def swap_dp(array):
        return lax.ppermute(array, "dp", [(0, 1), (1, 0)])

    def gathered(block):
        parts = [block] + [swap(block, 4 * r) for r in range(1, many)]
        return parts[0] if many == 1 else jnp.concatenate(parts, axis=0)

    index = lax.axis_index("expert").astype(jnp.int32)
    me = jnp.stack([index, lax.axis_index("dp").astype(jnp.int32)])
    held = Held()
    weights = lax.all_gather(expert_weights[0], "dp", axis=0, tiled=False)

    here_t, here_g = gathered(tokens), gathered(grad_out)
    held["t", 0], held["g", 0] = here_t, here_g
    near_t, near_g = swap(here_t, FLIP_NEAR), swap(here_g, FLIP_NEAR)
    far_t = swap(here_t, FLIP_FAR)

    key = jnp.where(slots >= 0, expert_ids * capacity + slots, -1)
    table = jnp.concatenate([key.T.astype(F32), gates.T], axis=0)
    held["tab"] = jnp.stack([table] + [swap(table, 4 * r) for r in range(1, many)])

    def table_of(c, which):
        return held["tabs"][which] if c == 0 else held["near tabs"][which] if c == 1 else (
            held["far tabs"][c - 2, which]
        )

    def send_full(c):
        held["t there", c] = swap(held["t", c], FLIP_Y)
        held["g there", c] = swap(held["g", c], FLIP_X)

    def pick_rows(c):
        here = table_of(c, 0)
        held["t own", c], sent_t = pick(
            me, FLIP_X, capacity, (here, table_of(c, 1)), held["t", c], held["t there", c]
        )
        held["g own", c], sent_g = pick(
            me, FLIP_Y, capacity, (here, table_of(c, 2)), held["g", c], held["g there", c]
        )
        held["t got", c] = swap(sent_t, FLIP_X)
        held["g got", c] = swap(sent_g, FLIP_Y)
        return sent_t, sent_g

    def run_expert(c):
        tables = jnp.concatenate([table_of(c, i) for i in range(3)] + [held["diagonal", c]])
        names = ("out own", "out sent", "back own", "back sent", "sums", "act", "dgate", "dup")
        rows = [held[n, c] for n in ("t own", "t got", "g own", "g got")]
        for name, value in zip(names, expert(me, capacity, tables, held["weights"], *rows)):
            held[name, c] = value

    def send_rows(c):
        held["out got", c] = swap(held["out sent", c], FLIP_X)
        held["back got", c] = swap(held["back sent", c], FLIP_Y)

    def sum_there(c):
        return (
            token_sum(me, FLIP_X, capacity, table_of(c, 1), held["out own", c], held["out got", c], 1),
            token_sum(me, FLIP_Y, capacity, table_of(c, 2), held["back own", c], held["back got", c], 1),
        )

    def send_parts(c, part_t, part_g):
        held["out part", c] = swap(part_t, FLIP_Y)
        held["back part", c] = swap(part_g, FLIP_X)

    def sum_here(c, mores=(), split=False):
        out, back = ([held[n + k, c] for k in (" own", " got", " part")] for n in ("out", "back"))
        return pair_sum(me, capacity, table_of(c, 0), out, back, mores, split)

    def sum_weights(left, names, reorder, at, before=()):
        pieces = [held[left + which, c] for c in range(CHUNKS) for which in (" own", " got")]
        rights = [[held[n, c] for c in range(CHUNKS)] for n in names]
        return weight_sums(me, pieces, rights, reorder, at, before)

    send_full(0)
    tab_x, tab_y = swap(held["tab"], FLIP_X), swap(held["tab"], FLIP_Y)
    held["tabs"] = jnp.stack([held["tab"], tab_y, tab_x])
    held.fence()
    sent = pick_rows(0)
    far_g = swap(after(here_g, near_t, near_g, far_t, *sent), FLIP_FAR)
    last_t, last_g = swap(after(far_t, near_t, near_g), FLIP_NEAR), swap(far_g, FLIP_NEAR)
    held["diagonal", 0] = swap(held["tabs"][1], FLIP_X)
    near_tabs = swap(held["tabs"], FLIP_NEAR)
    held["weights"] = weights
    held["t", 1], held["g", 1] = near_t, near_g
    held.fence()
    send_full(1)
    run_expert(0)
    held["near tabs"] = near_tabs
    held.fence()
    pick_rows(1)
    arrived = held["t got", 1], held["g got", 1]
    held["t", 2], held["g", 2] = after(far_t, *arrived), after(far_g, *arrived)
    send_full(2)
    held["t", 3], held["g", 3] = last_t, last_g
    held["diagonal", 1] = swap(held["near tabs"][1], FLIP_X)
    held["far tabs"] = swap(jnp.stack([held["tabs"], held["near tabs"]]), FLIP_FAR)
    held.fence()
    send_full(3)
    pick_rows(2)
    run_expert(1)
    diagonal = swap(held["far tabs"][:, 1], FLIP_X)
    held["diagonal", 2], held["diagonal", 3] = diagonal[0], diagonal[1]
    held.fence()
    pick_rows(3)
    run_expert(2)
    held.fence()
    send_rows(2)
    run_expert(3)
    held.fence()
    send_rows(3)
    held["part 2"] = sum_there(2)
    held.fence()
    held["weight sums"] = sum_weights("g", ["act"], True, 2)
    send_parts(3, *sum_there(3))
    sums = jnp.stack([held["sums", c] for c in range(CHUNKS)])
    sums = sums.reshape(CHUNKS, 2, 2, many, tok_count)
    held["sums"] = sums[:, 0], swap(sums[:, 1], FLIP_X)
    held.fence()
    held["weight sums"] = sum_weights("t", ["dgate", "dup"], False, 0, held["weight sums"])
    send_parts(2, *held["part 2"])
    send_rows(1)
    last = swap(sum_here(3), FLIP_NEAR)
    held["sum 2"] = sum_here(2, [last], True)
    sums = jnp.stack(held["sums"])
    held["sums"] = sums[:, :, 0], swap(sums[:, :, 1], FLIP_Y)
    held.fence()
    held["far t"] = swap(held["sum 2"][0], FLIP_FAR)
    send_parts(1, *sum_there(1))
    held["weights got"] = swap_dp(held["weight sums"][1])
    sums = jnp.stack(held["sums"])
    even = jnp.stack([sums[:, :, 0], sums[:, :, 2]])
    held["sums"] = even, swap(jnp.stack([sums[:, :, 1], sums[:, :, 3]]), FLIP_NEAR)
    held.fence()
    held["far g"] = swap(held["sum 2"][1], FLIP_FAR)
    held["near"] = swap(sum_here(1), FLIP_NEAR)
    send_rows(0)
    send_parts(0, *sum_there(0))
    weight_grads = held["weight sums"][0] + held["weights got"].astype(F32)
    held["weight grads"] = weight_grads.astype(BF16)[None]
    even, odd = held["sums"]
    held["sums"] = even[0], odd[0], swap(jnp.stack([even[1], odd[1]]), FLIP_FAR)
    held.fence()
    far = [held["far t"], held["far g"]]
    total_t, total_g = sum_here(0, [held["near"], far], True)
    here, near, far = held["sums"]
    sums = jnp.stack([here, near, far[0], far[1]])
    parts = [sums[:, :, :, 0]] + [swap(sums[:, :, :, r], 4 * r) for r in range(1, many)]
    sums = jnp.stack(parts, axis=1).reshape(n_expert, tok_count)
    source = jnp.arange(n_expert, dtype=jnp.int32) ^ index
    hit = (expert_ids[:, :, None] == source[None, None, :]) & (slots >= 0)[:, :, None]
    gate_grads = jnp.sum(jnp.where(hit, sums.T[:, None, :], 0.0), axis=2)

    def scattered(total):
        if many == 1:
            return total
        parts = [total[r * tok_count : (r + 1) * tok_count] for r in range(many)]
        result = parts[0].astype(F32)
        for r in range(1, many):
            result = result + swap(parts[r], 4 * r).astype(F32)
        return result.astype(BF16)

    return (
        scattered(total_t),
        gate_grads,
        scattered(total_g),
        held["weight grads"],
    )


def solution(mesh):
    placed = (
        P(("dp", "expert"), None),
        P(("dp", "expert"), None),
        P(("dp", "expert"), None),
        P(("dp", "expert"), None),
        P(("dp", "expert"), None),
        P("expert", None, None, "dp"),
    )
    return jax.shard_map(
        local,
        mesh=mesh,
        in_specs=placed,
        out_specs=(
            P(("dp", "expert"), None),
            P(("dp", "expert"), None),
            P(("dp", "expert"), None),
            P("expert", None, None, "dp"),
        ),
        check_vma=False,
    )
```

```python
import functools

import jax
import jax.numpy as jnp
from jax import lax
from jax.experimental import pallas as pl
from jax.experimental.pallas import tpu as pltpu
from jax.sharding import PartitionSpec as P

F32 = jnp.float32
BF16 = jnp.bfloat16
MIB = 1 << 20
CHUNKS = 4
HBM = pl.BlockSpec(memory_space=pl.ANY)
WHOLE = pl.BlockSpec(memory_space=pltpu.VMEM)
SCALAR = pl.BlockSpec(memory_space=pltpu.SMEM)


def mask_of(table, expert, capacity):
    top = table.shape[0] // 2
    tokens = table.shape[1]
    wanted = (expert * capacity + lax.broadcasted_iota(jnp.int32, (capacity, tokens), 0)).astype(F32)
    hit = jnp.zeros((capacity, tokens), F32)
    for k in range(top):
        hit = hit + jnp.where(table[k : k + 1] == wanted, 1.0, 0.0)
    return hit


def gate_column(table, expert, capacity):
    top = table.shape[0] // 2
    tokens = table.shape[1]
    wanted = (expert * capacity + lax.broadcasted_iota(jnp.int32, (capacity, tokens), 0)).astype(F32)
    gate = jnp.zeros((capacity, tokens), F32)
    for k in range(top):
        gate = gate + jnp.where(table[k : k + 1] == wanted, table[top + k : top + k + 1], 0.0)
    return jnp.sum(gate, axis=1, keepdims=True)


def pick_kernel(capacity, flip, blocks, n_deps, me_ref, *refs):
    tables, arrays = refs[:2], refs[2:4]
    own, sent = refs[4 + n_deps :]
    me = me_ref[0]
    for expert, out in ((me ^ flip, sent), (me, own)):
        for half in range(2):
            for b in range(blocks):
                mask = mask_of(tables[half][b], expert, capacity).astype(BF16)
                tokens = mask.shape[1]
                row = (half * blocks + b) * capacity
                source = arrays[half][b * tokens : (b + 1) * tokens, :]
                out[row : row + capacity, :] = jnp.dot(
                    mask, source, preferred_element_type=F32
                ).astype(BF16)


def pick(me, flip, capacity, tables, here, there, deps=()):
    blocks = tables[0].shape[0]
    in_rows, width = here.shape
    tile = 1024
    rows = 2 * blocks * capacity
    table_spec = pl.BlockSpec(tables[0].shape, lambda i: (0, 0, 0))
    in_spec = pl.BlockSpec((in_rows, tile), lambda i: (0, i))
    out_spec = pl.BlockSpec((rows, tile), lambda i: (0, i))
    return pl.pallas_call(
        functools.partial(pick_kernel, capacity, flip, blocks, len(deps)),
        grid=(width // tile,),
        in_specs=[SCALAR, table_spec, table_spec, in_spec, in_spec] + [HBM] * len(deps),
        out_specs=[out_spec] * 2,
        out_shape=[jax.ShapeDtypeStruct((rows, width), BF16)] * 2,
        compiler_params=pltpu.CompilerParams(vmem_limit_bytes=24 * MIB),
        cost_estimate=pl.CostEstimate(
            flops=8 * capacity * in_rows * width,
            bytes_accessed=4 * (in_rows + rows) * width,
            transcendentals=0,
        ),
        name="pick",
    )(me, *tables, here, there, *deps)


def expert_kernel(capacity, n_deps, me_ref, tables, weights, *refs):
    own_t, got_t, own_g, got_g = refs[:4]
    (out_own, out_sent, back_own, back_sent, gate_rows, act_out, dgate_out, dup_out) = refs[
        4 + n_deps : 12 + n_deps
    ]
    (w, x, g, gate_up, act_ref, dgate_ref, dup_ref, out, back, row_sem, w_sem, out_sem) = refs[
        12 + n_deps :
    ]
    half = weights.shape[3]
    hidden = 2 * half
    rows, width = x.shape
    side, quarter = rows // 2, rows // 4

    def started(source, target, sem):
        copy = pltpu.make_async_copy(source, target, sem)
        copy.start()
        return copy

    def row_quarters(q):
        return pl.ds(q * quarter, quarter)

    first, second = pl.ds(0, side), pl.ds(side, side)
    x_copies = [
        started(own_t, x.at[first], row_sem.at[0]),
        started(got_t, x.at[second], row_sem.at[1]),
    ]
    w_copies = [
        [started(weights.at[j, i], w.at[i, :, pl.ds(j * half, half)], w_sem.at[i, j]) for j in (0, 1)]
        for i in (0, 1)
    ]
    g_copies = [
        started(own_g.at[row_quarters(0)], g.at[row_quarters(0)], row_sem.at[2]),
        started(got_g.at[row_quarters(0)], g.at[row_quarters(1)], row_sem.at[3]),
        started(own_g.at[row_quarters(1)], g.at[row_quarters(2)], row_sem.at[4]),
        started(got_g.at[row_quarters(1)], g.at[row_quarters(3)], row_sem.at[5]),
    ]
    w_copies.append(
        [started(weights.at[j, 2], w.at[2, :, pl.ds(j * half, half)], w_sem.at[2, j]) for j in (0, 1)]
    )
    me = me_ref[0]
    groups = tables.shape[0]
    gates = jnp.concatenate(
        [gate_column(tables[i], me, capacity) for i in range(groups)], axis=0
    )
    step = 256

    def pre(i):
        def tile(n, carry):
            cols = pl.ds(pl.multiple_of(n * step, step), step)
            gate_up[i, :, cols] = jnp.dot(x[...], w[i, :, cols], preferred_element_type=F32)
            return carry

        lax.fori_loop(0, hidden // step, tile, 0, unroll=True)

    for copy in x_copies + w_copies[0]:
        copy.wait()
    pre(0)
    for copy in w_copies[1]:
        copy.wait()
    pre(1)
    for copy in g_copies + w_copies[2]:
        copy.wait()

    def hidden_tile(n, total):
        cols = pl.ds(pl.multiple_of(n * step, step), step)
        gate_pre, up_pre = gate_up[0, :, cols], gate_up[1, :, cols]
        pulled = jnp.dot(g[...], w[2, :, cols], preferred_element_type=F32)
        sig = jax.nn.sigmoid(gate_pre)
        silu = gate_pre * sig
        act = silu * up_pre
        grad_act = pulled * gates
        act_ref[:, cols] = (act * gates).astype(BF16)
        dgate_ref[:, cols] = (grad_act * up_pre * sig * (1.0 + gate_pre * (1.0 - sig))).astype(BF16)
        dup_ref[:, cols] = (grad_act * silu).astype(BF16)
        return total + jnp.sum(act * pulled, axis=1, keepdims=True)

    total = lax.fori_loop(0, hidden // step, hidden_tile, jnp.zeros((rows, 1), F32), unroll=True)
    copies = [
        started(act_ref, act_out, out_sem.at[0]),
        started(dgate_ref, dgate_out, out_sem.at[1]),
        started(dup_ref, dup_out, out_sem.at[2]),
    ]
    for i in range(groups):
        mask = mask_of(tables[i], me, capacity)
        gate_rows[i : i + 1, :] = jnp.sum(
            mask * total[i * capacity : (i + 1) * capacity], axis=0, keepdims=True
        )
    nt = (((1,), (1,)), ((), ()))

    def out_tile(n, carry):
        cols = pl.ds(pl.multiple_of(n * step, step), step)
        out[:, cols] = lax.dot_general(
            act_ref[...], w[2, cols, :], nt, preferred_element_type=F32
        ).astype(BF16)
        return carry

    def back_tile(n, carry):
        cols = pl.ds(pl.multiple_of(n * step, step), step)
        total = lax.dot_general(dgate_ref[...], w[0, cols, :], nt, preferred_element_type=F32)
        total += lax.dot_general(dup_ref[...], w[1, cols, :], nt, preferred_element_type=F32)
        back[:, cols] = total.astype(BF16)
        return carry

    lax.fori_loop(0, width // step, out_tile, 0, unroll=True)
    copies += [
        started(out.at[first], out_own, out_sem.at[3]),
        started(out.at[second], out_sent, out_sem.at[4]),
    ]
    lax.fori_loop(0, width // step, back_tile, 0, unroll=True)
    copies += [
        started(back.at[row_quarters(0)], back_own.at[row_quarters(0)], out_sem.at[5]),
        started(back.at[row_quarters(1)], back_sent.at[row_quarters(0)], out_sem.at[6]),
        started(back.at[row_quarters(2)], back_own.at[row_quarters(1)], out_sem.at[7]),
        started(back.at[row_quarters(3)], back_sent.at[row_quarters(1)], out_sem.at[8]),
    ]
    for copy in copies:
        copy.wait()


def expert(me, capacity, tables, weights, own_t, got_t, own_g, got_g, deps=()):
    rows, width = 2 * own_t.shape[0], own_t.shape[1]
    hidden = 2 * weights.shape[3]
    groups, _, tokens = tables.shape
    return pl.pallas_call(
        functools.partial(expert_kernel, capacity, len(deps)),
        in_specs=[SCALAR, WHOLE, HBM] + [HBM] * 4 + [HBM] * len(deps),
        out_specs=[HBM] * 4 + [WHOLE] + [HBM] * 3,
        out_shape=[jax.ShapeDtypeStruct((rows // 2, width), BF16)] * 4
        + [jax.ShapeDtypeStruct((groups, tokens), F32)]
        + [jax.ShapeDtypeStruct((rows, hidden), BF16)] * 3,
        scratch_shapes=[
            pltpu.VMEM((3, width, hidden), BF16),
            pltpu.VMEM((rows, width), BF16),
            pltpu.VMEM((rows, width), BF16),
            pltpu.VMEM((2, rows, hidden), F32),
            pltpu.VMEM((rows, hidden), BF16),
            pltpu.VMEM((rows, hidden), BF16),
            pltpu.VMEM((rows, hidden), BF16),
            pltpu.VMEM((rows, width), BF16),
            pltpu.VMEM((rows, width), BF16),
            pltpu.SemaphoreType.DMA((6,)),
            pltpu.SemaphoreType.DMA((3, 2)),
            pltpu.SemaphoreType.DMA((9,)),
        ],
        compiler_params=pltpu.CompilerParams(vmem_limit_bytes=60 * MIB),
        cost_estimate=pl.CostEstimate(
            flops=12 * rows * width * hidden,
            bytes_accessed=24 * width * hidden,
            transcendentals=rows * hidden,
        ),
        name="expert",
    )(me, tables, weights, own_t, got_t, own_g, got_g, *deps)


def sum_kernel(capacity, flip, n_other, n_deps, me_ref, tables, own, received, *refs):
    others, out = refs[:n_other], refs[n_other + n_deps]
    blocks, _, tokens = tables.shape
    me = me_ref[0]
    for b in range(blocks):
        here = slice(b * tokens, (b + 1) * tokens)
        slots = slice(b * capacity, (b + 1) * capacity)
        mask = jnp.concatenate(
            [mask_of(tables[b], me, capacity), mask_of(tables[b], me ^ flip, capacity)], axis=0
        )
        rows = jnp.concatenate([own[slots, :], received[slots, :]], axis=0)
        total = jnp.dot(mask.T.astype(BF16), rows, preferred_element_type=F32)
        for other in others:
            total = total + other[here, :].astype(F32)
        out[here, :] = total.astype(BF16)


def token_sum(me, flip, capacity, tables, own, received, half, others=(), deps=()):
    blocks, _, tokens = tables.shape
    width = own.shape[1]
    tile = 1024
    row_spec = pl.BlockSpec((blocks * capacity, tile), lambda i: (half, i))
    sum_spec = pl.BlockSpec((blocks * tokens, tile), lambda i: (0, i))
    return pl.pallas_call(
        functools.partial(sum_kernel, capacity, flip, len(others), len(deps)),
        grid=(width // tile,),
        in_specs=[SCALAR, pl.BlockSpec(tables.shape, lambda i: (0, 0, 0)), row_spec, row_spec]
        + [sum_spec] * len(others)
        + [HBM] * len(deps),
        out_specs=sum_spec,
        out_shape=jax.ShapeDtypeStruct((blocks * tokens, width), BF16),
        compiler_params=pltpu.CompilerParams(vmem_limit_bytes=24 * MIB),
        cost_estimate=pl.CostEstimate(
            flops=4 * blocks * tokens * capacity * width,
            bytes_accessed=2 * blocks * (tokens * (1 + len(others)) + 2 * capacity) * width,
            transcendentals=0,
        ),
        name="token_sum",
    )(me, tables, own, received, *others, *deps)


def there_kernel(capacity, me_ref, tables_t, tables_g, *refs):
    me = me_ref[0]
    for a, flip, tables in ((0, 1, tables_t), (1, 2, tables_g)):
        own, got = refs[2 * a : 2 * a + 2]
        blocks, _, tokens = tables.shape
        for b in range(blocks):
            slots = slice(b * capacity, (b + 1) * capacity)
            mask = jnp.concatenate(
                [mask_of(tables[b], me, capacity), mask_of(tables[b], me ^ flip, capacity)], axis=0
            )
            rows = jnp.concatenate([own[slots, :], got[slots, :]], axis=0)
            total = jnp.dot(mask.T.astype(BF16), rows, preferred_element_type=F32)
            refs[4 + a][b * tokens : (b + 1) * tokens, :] = total.astype(BF16)


def there_sum(me, capacity, tables_t, tables_g, out, back):
    blocks, _, tokens = tables_t.shape
    width = out[0].shape[1]
    tile = 1024
    rows = blocks * tokens
    table_spec = pl.BlockSpec(tables_t.shape, lambda i: (0, 0, 0))
    row_spec = pl.BlockSpec((blocks * capacity, tile), lambda i: (1, i))
    return pl.pallas_call(
        functools.partial(there_kernel, capacity),
        grid=(width // tile,),
        in_specs=[SCALAR, table_spec, table_spec] + [row_spec] * 4,
        out_specs=[pl.BlockSpec((rows, tile), lambda i: (0, i))] * 2,
        out_shape=[jax.ShapeDtypeStruct((rows, width), BF16)] * 2,
        compiler_params=pltpu.CompilerParams(vmem_limit_bytes=60 * MIB),
        cost_estimate=pl.CostEstimate(
            flops=8 * rows * capacity * width,
            bytes_accessed=4 * blocks * (tokens + 2 * capacity) * width,
            transcendentals=0,
        ),
        name="there_sum",
    )(me, tables_t, tables_g, *out, *back)


def pair_kernel(capacity, n_more, me_ref, tables, *refs):
    mores, outs = refs[6 : 6 + 2 * n_more], refs[6 + 2 * n_more :]
    blocks, _, tokens = tables.shape
    me = me_ref[0]
    for b in range(blocks):
        here = slice(b * tokens, (b + 1) * tokens)
        slots = slice(b * capacity, (b + 1) * capacity)
        mine = mask_of(tables[b], me, capacity)
        for a, flip in ((0, 1), (1, 2)):
            own, got, part = refs[3 * a : 3 * a + 3]
            mask = jnp.concatenate([mine, mask_of(tables[b], me ^ flip, capacity)], axis=0)
            rows = jnp.concatenate([own[slots, :], got[slots, :]], axis=0)
            total = jnp.dot(mask.T.astype(BF16), rows, preferred_element_type=F32)
            total = total + part[here, :].astype(F32)
            for more in mores[a::2]:
                total = total + more[here, :].astype(F32)
            if len(outs) == 1:
                outs[0][a, here, :] = total.astype(BF16)
            else:
                outs[a][here, :] = total.astype(BF16)


def pair_sum(me, capacity, tables, out, back, mores=(), split=False):
    blocks, _, tokens = tables.shape
    width = out[0].shape[1]
    tile = 1024
    rows = blocks * tokens
    row_spec = pl.BlockSpec((blocks * capacity, tile), lambda i: (0, i))
    sum_spec = pl.BlockSpec((rows, tile), lambda i: (0, i))
    pair_spec = pl.BlockSpec((2, rows, tile), lambda i: (0, 0, i))
    single = jax.ShapeDtypeStruct((rows, width), BF16)
    half_specs = [pl.BlockSpec((None, rows, tile), lambda i, a=a: (a, 0, i)) for a in range(2)]
    mores = [
        (m, [sum_spec] * 2) if isinstance(m, (list, tuple)) else ((m, m), half_specs) for m in mores
    ]
    result = pl.pallas_call(
        functools.partial(pair_kernel, capacity, len(mores)),
        grid=(width // tile,),
        in_specs=[SCALAR, pl.BlockSpec(tables.shape, lambda i: (0, 0, 0))]
        + [row_spec, row_spec, sum_spec] * 2
        + [s for _, specs in mores for s in specs],
        out_specs=[sum_spec] * 2 if split else pair_spec,
        out_shape=[single] * 2 if split else jax.ShapeDtypeStruct((2, rows, width), BF16),
        compiler_params=pltpu.CompilerParams(vmem_limit_bytes=60 * MIB),
        cost_estimate=pl.CostEstimate(
            flops=8 * rows * capacity * width,
            bytes_accessed=4 * blocks * (tokens * (2 + len(mores)) + 2 * capacity) * width,
            transcendentals=0,
        ),
        name="pair_sum",
    )(me, tables, *out, *back, *[m for pair, _ in mores for m in pair])
    return result


def weight_kernel(n_chunk, n_out, reorder, n_held, me_ref, *refs):
    left = jnp.concatenate([r[...] for r in refs[: 2 * n_chunk]], axis=0)
    rights = refs[2 * n_chunk : (2 + n_out) * n_chunk]
    own, other = refs[(2 + n_out) * n_chunk + n_held :]
    lower = me_ref[1] == 0
    tn = (((0,), (0,)), ((), ()))
    for i in range(n_out):
        parts = []
        for r in rights[i * n_chunk : (i + 1) * n_chunk]:
            quarter = r.shape[0] // 4
            for q in (0, 2, 1, 3) if reorder else range(4):
                parts.append(r[q * quarter : (q + 1) * quarter, :])
        right = jnp.concatenate(parts, axis=0)
        total = lax.dot_general(left, right, tn, preferred_element_type=F32)
        half = total.shape[1] // 2
        own[i] = jnp.where(lower, total[:, :half], total[:, half:])
        other[i] = jnp.where(lower, total[:, half:], total[:, :half]).astype(BF16)


def weight_sums(me, pieces, rights, reorder, at, before=()):
    width = pieces[0].shape[1]
    hidden = rights[0][0].shape[1]
    rows = sum(p.shape[0] for p in pieces)
    tile = 256
    n_out = len(rights)
    flat = [r for group in rights for r in group]
    n_in = 1 + len(pieces) + len(flat)
    return pl.pallas_call(
        functools.partial(weight_kernel, len(rights[0]), n_out, reorder, len(before)),
        grid=(width // tile,),
        in_specs=[SCALAR]
        + [pl.BlockSpec((p.shape[0], tile), lambda i: (0, i)) for p in pieces]
        + [pl.BlockSpec(r.shape, lambda i: (0, 0)) for r in flat]
        + [HBM] * len(before),
        out_specs=[pl.BlockSpec((n_out, tile, hidden // 2), lambda i: (at // n_out, i, 0))] * 2,
        out_shape=[
            jax.ShapeDtypeStruct((3, width, hidden // 2), F32),
            jax.ShapeDtypeStruct((3, width, hidden // 2), BF16),
        ],
        input_output_aliases={n_in + i: i for i in range(len(before))},
        compiler_params=pltpu.CompilerParams(vmem_limit_bytes=60 * MIB),
        cost_estimate=pl.CostEstimate(
            flops=2 * rows * width * hidden * n_out,
            bytes_accessed=n_out * 20 * width * hidden,
            transcendentals=0,
        ),
        name="weight_sums",
    )(me, *pieces, *flat, *before)


class Held(dict):
    def fence(self):
        names = list(self)
        for name, value in zip(names, lax.optimization_barrier([self[n] for n in names])):
            self[name] = value


def after(array, *deps):
    return lax.optimization_barrier((array, *deps))[0]


def local(tokens, gates, expert_ids, slots, grad_out, expert_weights):
    n_expert = lax.axis_size("expert")
    tok_count, top_count = expert_ids.shape
    capacity = tok_count * top_count // n_expert
    depth = n_expert // 4
    many = depth // CHUNKS
    FLIP_X, FLIP_Y, FLIP_NEAR, FLIP_FAR = 1, 2, 4 * many, 8 * many

    def swap(array, flip):
        return lax.ppermute(array, "expert", [(i, i ^ flip) for i in range(n_expert)])

    def swap_dp(array):
        return lax.ppermute(array, "dp", [(0, 1), (1, 0)])

    def gathered(block):
        parts = [block] + [swap(block, 4 * r) for r in range(1, many)]
        return parts[0] if many == 1 else jnp.concatenate(parts, axis=0)

    index = lax.axis_index("expert").astype(jnp.int32)
    me = jnp.stack([index, lax.axis_index("dp").astype(jnp.int32)])
    held = Held()
    weights = lax.all_gather(expert_weights[0], "dp", axis=0, tiled=False)

    here_t, here_g = gathered(tokens), gathered(grad_out)
    held["t", 0], held["g", 0] = here_t, here_g
    near_t, near_g = swap(here_t, FLIP_NEAR), swap(here_g, FLIP_NEAR)
    far_t = swap(here_t, FLIP_FAR)

    key = jnp.where(slots >= 0, expert_ids * capacity + slots, -1)
    table = jnp.concatenate([key.T.astype(F32), gates.T], axis=0)
    held["tab"] = jnp.stack([table] + [swap(table, 4 * r) for r in range(1, many)])

    def table_of(c, which):
        return held["tabs"][which] if c == 0 else held["near tabs"][which] if c == 1 else (
            held["far tabs"][c - 2, which]
        )

    def send_full(c):
        held["t there", c] = swap(held["t", c], FLIP_Y)
        held["g there", c] = swap(held["g", c], FLIP_X)

    def pick_rows(c):
        here = table_of(c, 0)
        held["t own", c], sent_t = pick(
            me, FLIP_X, capacity, (here, table_of(c, 1)), held["t", c], held["t there", c]
        )
        held["g own", c], sent_g = pick(
            me, FLIP_Y, capacity, (here, table_of(c, 2)), held["g", c], held["g there", c]
        )
        held["t got", c] = swap(sent_t, FLIP_X)
        held["g got", c] = swap(sent_g, FLIP_Y)
        return sent_t, sent_g

    def run_expert(c):
        tables = jnp.concatenate([table_of(c, i) for i in range(4)])
        names = ("out own", "out sent", "back own", "back sent", "sums", "act", "dgate", "dup")
        rows = [held[n, c] for n in ("t own", "t got", "g own", "g got")]
        for name, value in zip(names, expert(me, capacity, tables, held["weights"], *rows)):
            held[name, c] = value

    def send_rows(c):
        held["out got", c] = swap(held["out sent", c], FLIP_X)
        held["back got", c] = swap(held["back sent", c], FLIP_Y)

    def sum_there(c):
        out, back = ([held[n + k, c] for k in (" own", " got")] for n in ("out", "back"))
        return there_sum(me, capacity, table_of(c, 1), table_of(c, 2), out, back)

    def send_parts(c, part_t, part_g):
        held["out part", c] = swap(part_t, FLIP_Y)
        held["back part", c] = swap(part_g, FLIP_X)

    def sum_here(c, mores=(), split=False):
        out, back = ([held[n + k, c] for k in (" own", " got", " part")] for n in ("out", "back"))
        return pair_sum(me, capacity, table_of(c, 0), out, back, mores, split)

    def sum_weights(left, names, reorder, at, before=()):
        pieces = [held[left + which, c] for c in range(CHUNKS) for which in (" own", " got")]
        rights = [[held[n, c] for c in range(CHUNKS)] for n in names]
        return weight_sums(me, pieces, rights, reorder, at, before)

    send_full(0)
    held.fence()
    tab_x, tab_y = swap(held["tab"], FLIP_X), swap(held["tab"], FLIP_Y)
    held["tabs"] = jnp.stack([held["tab"], tab_y, tab_x])
    held.fence()
    pick_rows(0)
    diagonal = swap(held["tabs"][1], FLIP_X)
    held["tabs"] = jnp.concatenate([held["tabs"], diagonal[None]])
    held["weights"] = weights
    held["t", 1], held["g", 1], held["t", 2] = near_t, near_g, far_t
    held.fence()
    send_full(1)
    held["near tabs"] = swap(held["tabs"], FLIP_NEAR)
    far_g = swap(held["g", 0], FLIP_FAR)
    held.fence()
    sent = pick_rows(1)
    held["g", 2] = after(far_g, *sent)
    send_full(2)
    run_expert(0)
    last_g = swap(held["g", 2], FLIP_NEAR)
    held["far tabs"] = swap(jnp.stack([held["tabs"], held["near tabs"]]), FLIP_FAR)
    held["t", 3] = swap(after(held["t", 2], held["far tabs"], *sent), FLIP_NEAR)
    held.fence()
    sent = pick_rows(2)
    held["g", 3] = after(last_g, *sent)
    send_full(3)
    run_expert(1)
    held.fence()
    send_rows(1)
    pick_rows(3)
    run_expert(2)
    held.fence()
    send_rows(2)
    run_expert(3)
    held.fence()
    send_rows(3)
    held["part 2"] = sum_there(2)
    sums = jnp.stack([held["sums", c] for c in range(CHUNKS)])
    sums = sums.reshape(CHUNKS, 2, 2, many, tok_count)
    held["sums"] = sums[:, 0], swap(sums[:, 1], FLIP_X)
    held.fence()
    send_parts(3, *sum_there(3))
    sums = jnp.stack(held["sums"])
    held["sums"] = sums[:, :, 0], swap(sums[:, :, 1], FLIP_Y)
    held.fence()
    total = sum_here(3)
    held["part 2"] = [after(part, total) for part in held["part 2"]]
    send_parts(2, *held["part 2"])
    last = swap(total, FLIP_NEAR)
    send_parts(1, *sum_there(1))
    held["weight sums"] = sum_weights("t", ["dgate", "dup"], False, 0)
    held["sum 2"] = sum_here(2, [last], True)
    held.fence()
    held["far t"] = swap(held["sum 2"][0], FLIP_FAR)
    total_t, held["sum 1"] = sum_here(1, [], True)
    held["near t"] = swap(total_t, FLIP_NEAR)
    for name in (("out sent", 0), ("back sent", 0)):
        held[name] = after(held[name], total_t)
    send_rows(0)
    held["part 0"] = sum_there(0)
    held["weight sums"] = sum_weights("g", ["act"], True, 2, held["weight sums"])
    sums = jnp.stack(held["sums"])
    beyond = swap(after(sums[:, :, 2:], held["out got", 0], held["back got", 0]), FLIP_FAR)
    held["sums"] = sums[:, :, :2], beyond
    held.fence()

    def last_sum(name, flip, which):
        rows = (held[name + k, 0] for k in (" own", " got"))
        others = held[name + " part", 0], held["near " + which], held["far " + which]
        return token_sum(me, flip, capacity, table_of(0, 0), *rows, 0, others)

    held["far g"] = swap(held["sum 2"][1], FLIP_FAR)
    held["near g"] = swap(held["sum 1"], FLIP_NEAR)
    send_parts(0, *held["part 0"])
    weights_got = swap_dp(held["weight sums"][1])
    weight_grads = held["weight sums"][0] + weights_got.astype(F32)
    held["weight grads"] = weight_grads.astype(BF16)[None]
    held["total t"] = last_sum("out", FLIP_X, "t")
    sums = jnp.stack(held["sums"])
    beside = swap(after(sums[:, :, :, 1], held["total t"]), FLIP_NEAR)
    held["sums"] = sums[:, :, :, 0], beside
    held.fence()
    total_t, total_g = held["total t"], last_sum("back", FLIP_Y, "g")
    sums = jnp.stack(held["sums"], axis=1).reshape(CHUNKS, 2, 2, many, tok_count)
    parts = [sums[:, :, :, 0]] + [swap(sums[:, :, :, r], 4 * r) for r in range(1, many)]
    sums = jnp.stack(parts, axis=1).reshape(n_expert, tok_count)
    source = jnp.arange(n_expert, dtype=jnp.int32) ^ index
    hit = (expert_ids[:, :, None] == source[None, None, :]) & (slots >= 0)[:, :, None]
    gate_grads = jnp.sum(jnp.where(hit, sums.T[:, None, :], 0.0), axis=2)

    def scattered(total):
        if many == 1:
            return total
        parts = [total[r * tok_count : (r + 1) * tok_count] for r in range(many)]
        result = parts[0].astype(F32)
        for r in range(1, many):
            result = result + swap(parts[r], 4 * r).astype(F32)
        return result.astype(BF16)

    return (
        scattered(total_t),
        gate_grads,
        scattered(total_g),
        held["weight grads"],
    )


def solution(mesh):
    placed = (
        P(("dp", "expert"), None),
        P(("dp", "expert"), None),
        P(("dp", "expert"), None),
        P(("dp", "expert"), None),
        P(("dp", "expert"), None),
        P("expert", None, None, "dp"),
    )
    return jax.shard_map(
        local,
        mesh=mesh,
        in_specs=placed,
        out_specs=(
            P(("dp", "expert"), None),
            P(("dp", "expert"), None),
            P(("dp", "expert"), None),
            P("expert", None, None, "dp"),
        ),
        check_vma=False,
    )
```

```python
import functools

import jax
import jax.numpy as jnp
from jax import lax
from jax.experimental import pallas as pl
from jax.experimental.pallas import tpu as pltpu
from jax.sharding import PartitionSpec as P

F32 = jnp.float32
BF16 = jnp.bfloat16
MIB = 1 << 20
CHUNKS = 4
HBM = pl.BlockSpec(memory_space=pl.ANY)
WHOLE = pl.BlockSpec(memory_space=pltpu.VMEM)
SCALAR = pl.BlockSpec(memory_space=pltpu.SMEM)


def mask_of(table, expert, capacity):
    top = table.shape[0] // 2
    tokens = table.shape[1]
    wanted = (expert * capacity + lax.broadcasted_iota(jnp.int32, (capacity, tokens), 0)).astype(F32)
    hit = jnp.zeros((capacity, tokens), F32)
    for k in range(top):
        hit = hit + jnp.where(table[k : k + 1] == wanted, 1.0, 0.0)
    return hit


def gate_column(table, expert, capacity):
    top = table.shape[0] // 2
    tokens = table.shape[1]
    wanted = (expert * capacity + lax.broadcasted_iota(jnp.int32, (capacity, tokens), 0)).astype(F32)
    gate = jnp.zeros((capacity, tokens), F32)
    for k in range(top):
        gate = gate + jnp.where(table[k : k + 1] == wanted, table[top + k : top + k + 1], 0.0)
    return jnp.sum(gate, axis=1, keepdims=True)


def pick_kernel(capacity, flip, blocks, n_deps, me_ref, *refs):
    tables, arrays = refs[:2], refs[2:4]
    own, sent = refs[4 + n_deps :]
    me = me_ref[0]
    for expert, out in ((me ^ flip, sent), (me, own)):
        for half in range(2):
            for b in range(blocks):
                mask = mask_of(tables[half][b], expert, capacity).astype(BF16)
                tokens = mask.shape[1]
                row = (half * blocks + b) * capacity
                source = arrays[half][b * tokens : (b + 1) * tokens, :]
                out[row : row + capacity, :] = jnp.dot(
                    mask, source, preferred_element_type=F32
                ).astype(BF16)


def pick(me, flip, capacity, tables, here, there, deps=()):
    blocks = tables[0].shape[0]
    in_rows, width = here.shape
    tile = 1024
    rows = 2 * blocks * capacity
    table_spec = pl.BlockSpec(tables[0].shape, lambda i: (0, 0, 0))
    in_spec = pl.BlockSpec((in_rows, tile), lambda i: (0, i))
    out_spec = pl.BlockSpec((rows, tile), lambda i: (0, i))
    return pl.pallas_call(
        functools.partial(pick_kernel, capacity, flip, blocks, len(deps)),
        grid=(width // tile,),
        in_specs=[SCALAR, table_spec, table_spec, in_spec, in_spec] + [HBM] * len(deps),
        out_specs=[out_spec] * 2,
        out_shape=[jax.ShapeDtypeStruct((rows, width), BF16)] * 2,
        compiler_params=pltpu.CompilerParams(vmem_limit_bytes=24 * MIB),
        cost_estimate=pl.CostEstimate(
            flops=8 * capacity * in_rows * width,
            bytes_accessed=4 * (in_rows + rows) * width,
            transcendentals=0,
        ),
        name="pick",
    )(me, *tables, here, there, *deps)


def expert_kernel(capacity, n_deps, me_ref, tables, weights, *refs):
    own_t, got_t, own_g, got_g = refs[:4]
    (out_own, out_sent, back_own, back_sent, gate_rows, act_out, dgate_out, dup_out) = refs[
        4 + n_deps : 12 + n_deps
    ]
    (w, x, g, gate_up, act_ref, dgate_ref, dup_ref, out, back, row_sem, w_sem, out_sem) = refs[
        12 + n_deps :
    ]
    half = weights.shape[3]
    hidden = 2 * half
    rows, width = x.shape
    side, quarter = rows // 2, rows // 4

    def started(source, target, sem):
        copy = pltpu.make_async_copy(source, target, sem)
        copy.start()
        return copy

    def row_quarters(q):
        return pl.ds(q * quarter, quarter)

    first, second = pl.ds(0, side), pl.ds(side, side)
    x_copies = [
        started(own_t, x.at[first], row_sem.at[0]),
        started(got_t, x.at[second], row_sem.at[1]),
    ]
    w_copies = [
        [started(weights.at[j, i], w.at[i, :, pl.ds(j * half, half)], w_sem.at[i, j]) for j in (0, 1)]
        for i in (0, 1)
    ]
    g_copies = [
        started(own_g.at[row_quarters(0)], g.at[row_quarters(0)], row_sem.at[2]),
        started(got_g.at[row_quarters(0)], g.at[row_quarters(1)], row_sem.at[3]),
        started(own_g.at[row_quarters(1)], g.at[row_quarters(2)], row_sem.at[4]),
        started(got_g.at[row_quarters(1)], g.at[row_quarters(3)], row_sem.at[5]),
    ]
    w_copies.append(
        [started(weights.at[j, 2], w.at[2, :, pl.ds(j * half, half)], w_sem.at[2, j]) for j in (0, 1)]
    )
    me = me_ref[0]
    groups = tables.shape[0]
    gates = jnp.concatenate(
        [gate_column(tables[i], me, capacity) for i in range(groups)], axis=0
    )
    step = 256

    def pre(i):
        def tile(n, carry):
            cols = pl.ds(pl.multiple_of(n * step, step), step)
            gate_up[i, :, cols] = jnp.dot(x[...], w[i, :, cols], preferred_element_type=F32)
            return carry

        lax.fori_loop(0, hidden // step, tile, 0, unroll=True)

    for copy in x_copies + w_copies[0]:
        copy.wait()
    pre(0)
    for copy in w_copies[1]:
        copy.wait()
    pre(1)
    for copy in g_copies + w_copies[2]:
        copy.wait()

    def hidden_tile(n, total):
        cols = pl.ds(pl.multiple_of(n * step, step), step)
        gate_pre, up_pre = gate_up[0, :, cols], gate_up[1, :, cols]
        pulled = jnp.dot(g[...], w[2, :, cols], preferred_element_type=F32)
        sig = jax.nn.sigmoid(gate_pre)
        silu = gate_pre * sig
        act = silu * up_pre
        grad_act = pulled * gates
        act_ref[:, cols] = (act * gates).astype(BF16)
        dgate_ref[:, cols] = (grad_act * up_pre * sig * (1.0 + gate_pre * (1.0 - sig))).astype(BF16)
        dup_ref[:, cols] = (grad_act * silu).astype(BF16)
        return total + jnp.sum(act * pulled, axis=1, keepdims=True)

    total = lax.fori_loop(0, hidden // step, hidden_tile, jnp.zeros((rows, 1), F32), unroll=True)
    copies = [
        started(act_ref, act_out, out_sem.at[0]),
        started(dgate_ref, dgate_out, out_sem.at[1]),
        started(dup_ref, dup_out, out_sem.at[2]),
    ]
    for i in range(groups):
        mask = mask_of(tables[i], me, capacity)
        gate_rows[i : i + 1, :] = jnp.sum(
            mask * total[i * capacity : (i + 1) * capacity], axis=0, keepdims=True
        )
    nt = (((1,), (1,)), ((), ()))

    def out_tile(n, carry):
        cols = pl.ds(pl.multiple_of(n * step, step), step)
        out[:, cols] = lax.dot_general(
            act_ref[...], w[2, cols, :], nt, preferred_element_type=F32
        ).astype(BF16)
        return carry

    def back_tile(n, carry):
        cols = pl.ds(pl.multiple_of(n * step, step), step)
        total = lax.dot_general(dgate_ref[...], w[0, cols, :], nt, preferred_element_type=F32)
        total += lax.dot_general(dup_ref[...], w[1, cols, :], nt, preferred_element_type=F32)
        back[:, cols] = total.astype(BF16)
        return carry

    lax.fori_loop(0, width // step, out_tile, 0, unroll=True)
    copies += [
        started(out.at[first], out_own, out_sem.at[3]),
        started(out.at[second], out_sent, out_sem.at[4]),
    ]
    lax.fori_loop(0, width // step, back_tile, 0, unroll=True)
    copies += [
        started(back.at[row_quarters(0)], back_own.at[row_quarters(0)], out_sem.at[5]),
        started(back.at[row_quarters(1)], back_sent.at[row_quarters(0)], out_sem.at[6]),
        started(back.at[row_quarters(2)], back_own.at[row_quarters(1)], out_sem.at[7]),
        started(back.at[row_quarters(3)], back_sent.at[row_quarters(1)], out_sem.at[8]),
    ]
    for copy in copies:
        copy.wait()


def expert(me, capacity, tables, weights, own_t, got_t, own_g, got_g, deps=()):
    rows, width = 2 * own_t.shape[0], own_t.shape[1]
    hidden = 2 * weights.shape[3]
    groups, _, tokens = tables.shape
    return pl.pallas_call(
        functools.partial(expert_kernel, capacity, len(deps)),
        in_specs=[SCALAR, WHOLE, HBM] + [HBM] * 4 + [HBM] * len(deps),
        out_specs=[HBM] * 4 + [WHOLE] + [HBM] * 3,
        out_shape=[jax.ShapeDtypeStruct((rows // 2, width), BF16)] * 4
        + [jax.ShapeDtypeStruct((groups, tokens), F32)]
        + [jax.ShapeDtypeStruct((rows, hidden), BF16)] * 3,
        scratch_shapes=[
            pltpu.VMEM((3, width, hidden), BF16),
            pltpu.VMEM((rows, width), BF16),
            pltpu.VMEM((rows, width), BF16),
            pltpu.VMEM((2, rows, hidden), F32),
            pltpu.VMEM((rows, hidden), BF16),
            pltpu.VMEM((rows, hidden), BF16),
            pltpu.VMEM((rows, hidden), BF16),
            pltpu.VMEM((rows, width), BF16),
            pltpu.VMEM((rows, width), BF16),
            pltpu.SemaphoreType.DMA((6,)),
            pltpu.SemaphoreType.DMA((3, 2)),
            pltpu.SemaphoreType.DMA((9,)),
        ],
        compiler_params=pltpu.CompilerParams(vmem_limit_bytes=60 * MIB),
        cost_estimate=pl.CostEstimate(
            flops=12 * rows * width * hidden,
            bytes_accessed=24 * width * hidden,
            transcendentals=rows * hidden,
        ),
        name="expert",
    )(me, tables, weights, own_t, got_t, own_g, got_g, *deps)


def sum_kernel(capacity, flip, n_other, n_deps, me_ref, tables, own, received, *refs):
    others, out = refs[:n_other], refs[n_other + n_deps]
    blocks, _, tokens = tables.shape
    me = me_ref[0]
    for b in range(blocks):
        here = slice(b * tokens, (b + 1) * tokens)
        slots = slice(b * capacity, (b + 1) * capacity)
        mask = jnp.concatenate(
            [mask_of(tables[b], me, capacity), mask_of(tables[b], me ^ flip, capacity)], axis=0
        )
        rows = jnp.concatenate([own[slots, :], received[slots, :]], axis=0)
        total = jnp.dot(mask.T.astype(BF16), rows, preferred_element_type=F32)
        for other in others:
            total = total + other[here, :].astype(F32)
        out[here, :] = total.astype(BF16)


def token_sum(me, flip, capacity, tables, own, received, half, others=(), deps=()):
    blocks, _, tokens = tables.shape
    width = own.shape[1]
    tile = 1024
    row_spec = pl.BlockSpec((blocks * capacity, tile), lambda i: (half, i))
    sum_spec = pl.BlockSpec((blocks * tokens, tile), lambda i: (0, i))
    return pl.pallas_call(
        functools.partial(sum_kernel, capacity, flip, len(others), len(deps)),
        grid=(width // tile,),
        in_specs=[SCALAR, pl.BlockSpec(tables.shape, lambda i: (0, 0, 0)), row_spec, row_spec]
        + [sum_spec] * len(others)
        + [HBM] * len(deps),
        out_specs=sum_spec,
        out_shape=jax.ShapeDtypeStruct((blocks * tokens, width), BF16),
        compiler_params=pltpu.CompilerParams(vmem_limit_bytes=24 * MIB),
        cost_estimate=pl.CostEstimate(
            flops=4 * blocks * tokens * capacity * width,
            bytes_accessed=2 * blocks * (tokens * (1 + len(others)) + 2 * capacity) * width,
            transcendentals=0,
        ),
        name="token_sum",
    )(me, tables, own, received, *others, *deps)


def there_kernel(capacity, me_ref, tables_t, tables_g, *refs):
    me = me_ref[0]
    for a, flip, tables in ((0, 1, tables_t), (1, 2, tables_g)):
        own, got = refs[2 * a : 2 * a + 2]
        blocks, _, tokens = tables.shape
        for b in range(blocks):
            slots = slice(b * capacity, (b + 1) * capacity)
            mask = jnp.concatenate(
                [mask_of(tables[b], me, capacity), mask_of(tables[b], me ^ flip, capacity)], axis=0
            )
            rows = jnp.concatenate([own[slots, :], got[slots, :]], axis=0)
            total = jnp.dot(mask.T.astype(BF16), rows, preferred_element_type=F32)
            refs[4 + a][b * tokens : (b + 1) * tokens, :] = total.astype(BF16)


def there_sum(me, capacity, tables_t, tables_g, out, back):
    blocks, _, tokens = tables_t.shape
    width = out[0].shape[1]
    tile = 1024
    rows = blocks * tokens
    table_spec = pl.BlockSpec(tables_t.shape, lambda i: (0, 0, 0))
    row_spec = pl.BlockSpec((blocks * capacity, tile), lambda i: (1, i))
    return pl.pallas_call(
        functools.partial(there_kernel, capacity),
        grid=(width // tile,),
        in_specs=[SCALAR, table_spec, table_spec] + [row_spec] * 4,
        out_specs=[pl.BlockSpec((rows, tile), lambda i: (0, i))] * 2,
        out_shape=[jax.ShapeDtypeStruct((rows, width), BF16)] * 2,
        compiler_params=pltpu.CompilerParams(vmem_limit_bytes=60 * MIB),
        cost_estimate=pl.CostEstimate(
            flops=8 * rows * capacity * width,
            bytes_accessed=4 * blocks * (tokens + 2 * capacity) * width,
            transcendentals=0,
        ),
        name="there_sum",
    )(me, tables_t, tables_g, *out, *back)


def pair_kernel(capacity, n_more, me_ref, tables, *refs):
    mores, outs = refs[6 : 6 + 2 * n_more], refs[6 + 2 * n_more :]
    blocks, _, tokens = tables.shape
    me = me_ref[0]
    for b in range(blocks):
        here = slice(b * tokens, (b + 1) * tokens)
        slots = slice(b * capacity, (b + 1) * capacity)
        mine = mask_of(tables[b], me, capacity)
        for a, flip in ((0, 1), (1, 2)):
            own, got, part = refs[3 * a : 3 * a + 3]
            mask = jnp.concatenate([mine, mask_of(tables[b], me ^ flip, capacity)], axis=0)
            rows = jnp.concatenate([own[slots, :], got[slots, :]], axis=0)
            total = jnp.dot(mask.T.astype(BF16), rows, preferred_element_type=F32)
            total = total + part[here, :].astype(F32)
            for more in mores[a::2]:
                total = total + more[here, :].astype(F32)
            if len(outs) == 1:
                outs[0][a, here, :] = total.astype(BF16)
            else:
                outs[a][here, :] = total.astype(BF16)


def pair_sum(me, capacity, tables, out, back, mores=(), split=False):
    blocks, _, tokens = tables.shape
    width = out[0].shape[1]
    tile = 1024
    rows = blocks * tokens
    row_spec = pl.BlockSpec((blocks * capacity, tile), lambda i: (0, i))
    sum_spec = pl.BlockSpec((rows, tile), lambda i: (0, i))
    pair_spec = pl.BlockSpec((2, rows, tile), lambda i: (0, 0, i))
    single = jax.ShapeDtypeStruct((rows, width), BF16)
    half_specs = [pl.BlockSpec((None, rows, tile), lambda i, a=a: (a, 0, i)) for a in range(2)]
    mores = [
        (m, [sum_spec] * 2) if isinstance(m, (list, tuple)) else ((m, m), half_specs) for m in mores
    ]
    result = pl.pallas_call(
        functools.partial(pair_kernel, capacity, len(mores)),
        grid=(width // tile,),
        in_specs=[SCALAR, pl.BlockSpec(tables.shape, lambda i: (0, 0, 0))]
        + [row_spec, row_spec, sum_spec] * 2
        + [s for _, specs in mores for s in specs],
        out_specs=[sum_spec] * 2 if split else pair_spec,
        out_shape=[single] * 2 if split else jax.ShapeDtypeStruct((2, rows, width), BF16),
        compiler_params=pltpu.CompilerParams(vmem_limit_bytes=60 * MIB),
        cost_estimate=pl.CostEstimate(
            flops=8 * rows * capacity * width,
            bytes_accessed=4 * blocks * (tokens * (2 + len(mores)) + 2 * capacity) * width,
            transcendentals=0,
        ),
        name="pair_sum",
    )(me, tables, *out, *back, *[m for pair, _ in mores for m in pair])
    return result


def weight_kernel(n_chunk, n_out, reorder, n_held, me_ref, *refs):
    left = jnp.concatenate([r[...] for r in refs[: 2 * n_chunk]], axis=0)
    rights = refs[2 * n_chunk : (2 + n_out) * n_chunk]
    own, other = refs[(2 + n_out) * n_chunk + n_held :]
    lower = me_ref[1] == 0
    tn = (((0,), (0,)), ((), ()))
    for i in range(n_out):
        parts = []
        for r in rights[i * n_chunk : (i + 1) * n_chunk]:
            quarter = r.shape[0] // 4
            for q in (0, 2, 1, 3) if reorder else range(4):
                parts.append(r[q * quarter : (q + 1) * quarter, :])
        right = jnp.concatenate(parts, axis=0)
        total = lax.dot_general(left, right, tn, preferred_element_type=F32)
        half = total.shape[1] // 2
        own[i] = jnp.where(lower, total[:, :half], total[:, half:])
        other[i] = jnp.where(lower, total[:, half:], total[:, :half]).astype(BF16)


def weight_sums(me, pieces, rights, reorder, at, before=()):
    width = pieces[0].shape[1]
    hidden = rights[0][0].shape[1]
    rows = sum(p.shape[0] for p in pieces)
    tile = 256
    n_out = len(rights)
    flat = [r for group in rights for r in group]
    n_in = 1 + len(pieces) + len(flat)
    return pl.pallas_call(
        functools.partial(weight_kernel, len(rights[0]), n_out, reorder, len(before)),
        grid=(width // tile,),
        in_specs=[SCALAR]
        + [pl.BlockSpec((p.shape[0], tile), lambda i: (0, i)) for p in pieces]
        + [pl.BlockSpec(r.shape, lambda i: (0, 0)) for r in flat]
        + [HBM] * len(before),
        out_specs=[pl.BlockSpec((n_out, tile, hidden // 2), lambda i: (at // n_out, i, 0))] * 2,
        out_shape=[
            jax.ShapeDtypeStruct((3, width, hidden // 2), F32),
            jax.ShapeDtypeStruct((3, width, hidden // 2), BF16),
        ],
        input_output_aliases={n_in + i: i for i in range(len(before))},
        compiler_params=pltpu.CompilerParams(vmem_limit_bytes=60 * MIB),
        cost_estimate=pl.CostEstimate(
            flops=2 * rows * width * hidden * n_out,
            bytes_accessed=n_out * 20 * width * hidden,
            transcendentals=0,
        ),
        name="weight_sums",
    )(me, *pieces, *flat, *before)


class Held(dict):
    def fence(self):
        names = list(self)
        for name, value in zip(names, lax.optimization_barrier([self[n] for n in names])):
            self[name] = value


def after(array, *deps):
    return lax.optimization_barrier((array, *deps))[0]


def local(tokens, gates, expert_ids, slots, grad_out, expert_weights):
    n_expert = lax.axis_size("expert")
    tok_count, top_count = expert_ids.shape
    capacity = tok_count * top_count // n_expert
    depth = n_expert // 4
    many = depth // CHUNKS
    FLIP_X, FLIP_Y, FLIP_NEAR, FLIP_FAR = 1, 2, 4 * many, 8 * many

    def swap(array, flip):
        return lax.ppermute(array, "expert", [(i, i ^ flip) for i in range(n_expert)])

    def swap_dp(array):
        return lax.ppermute(array, "dp", [(0, 1), (1, 0)])

    def gathered(block):
        parts = [block] + [swap(block, 4 * r) for r in range(1, many)]
        return parts[0] if many == 1 else jnp.concatenate(parts, axis=0)

    index = lax.axis_index("expert").astype(jnp.int32)
    me = jnp.stack([index, lax.axis_index("dp").astype(jnp.int32)])
    held = Held()
    weights = lax.all_gather(expert_weights[0], "dp", axis=0, tiled=False)

    here_t, here_g = gathered(tokens), gathered(grad_out)
    held["t", 0], held["g", 0] = here_t, here_g
    near_t, near_g = swap(here_t, FLIP_NEAR), swap(here_g, FLIP_NEAR)
    far_t = swap(here_t, FLIP_FAR)

    key = jnp.where(slots >= 0, expert_ids * capacity + slots, -1)
    table = jnp.concatenate([key.T.astype(F32), gates.T], axis=0)
    held["tab"] = jnp.stack([table] + [swap(table, 4 * r) for r in range(1, many)])

    def table_of(c, which):
        return held["tabs"][which] if c == 0 else held["near tabs"][which] if c == 1 else (
            held["far tabs"][c - 2, which]
        )

    def send_full(c):
        held["t there", c] = swap(held["t", c], FLIP_Y)
        held["g there", c] = swap(held["g", c], FLIP_X)

    def pick_rows(c):
        here = table_of(c, 0)
        held["t own", c], sent_t = pick(
            me, FLIP_X, capacity, (here, table_of(c, 1)), held["t", c], held["t there", c]
        )
        held["g own", c], sent_g = pick(
            me, FLIP_Y, capacity, (here, table_of(c, 2)), held["g", c], held["g there", c]
        )
        held["t got", c] = swap(sent_t, FLIP_X)
        held["g got", c] = swap(sent_g, FLIP_Y)
        return sent_t, sent_g

    def run_expert(c):
        tables = jnp.concatenate([table_of(c, i) for i in range(4)])
        names = ("out own", "out sent", "back own", "back sent", "sums", "act", "dgate", "dup")
        rows = [held[n, c] for n in ("t own", "t got", "g own", "g got")]
        for name, value in zip(names, expert(me, capacity, tables, held["weights"], *rows)):
            held[name, c] = value

    def send_rows(c):
        held["out got", c] = swap(held["out sent", c], FLIP_X)
        held["back got", c] = swap(held["back sent", c], FLIP_Y)

    def sum_there(c):
        out, back = ([held[n + k, c] for k in (" own", " got")] for n in ("out", "back"))
        return there_sum(me, capacity, table_of(c, 1), table_of(c, 2), out, back)

    def send_parts(c, part_t, part_g):
        held["out part", c] = swap(part_t, FLIP_Y)
        held["back part", c] = swap(part_g, FLIP_X)

    def sum_here(c, mores=(), split=False):
        out, back = ([held[n + k, c] for k in (" own", " got", " part")] for n in ("out", "back"))
        return pair_sum(me, capacity, table_of(c, 0), out, back, mores, split)

    def sum_weights(left, names, reorder, at, before=()):
        pieces = [held[left + which, c] for c in range(CHUNKS) for which in (" own", " got")]
        rights = [[held[n, c] for c in range(CHUNKS)] for n in names]
        return weight_sums(me, pieces, rights, reorder, at, before)

    send_full(0)
    held.fence()
    tab_x, tab_y = swap(held["tab"], FLIP_X), swap(held["tab"], FLIP_Y)
    held["tabs"] = jnp.stack([held["tab"], tab_y, tab_x])
    held.fence()
    pick_rows(0)
    diagonal = swap(held["tabs"][1], FLIP_X)
    held["tabs"] = jnp.concatenate([held["tabs"], diagonal[None]])
    held["weights"] = weights
    held["t", 1], held["g", 1], held["t", 2] = near_t, near_g, far_t
    held.fence()
    send_full(1)
    held["near tabs"] = swap(held["tabs"], FLIP_NEAR)
    far_g = swap(held["g", 0], FLIP_FAR)
    held.fence()
    sent = pick_rows(1)
    held["g", 2] = after(far_g, *sent)
    send_full(2)
    run_expert(0)
    last_g = swap(held["g", 2], FLIP_NEAR)
    held["far tabs"] = swap(jnp.stack([held["tabs"], held["near tabs"]]), FLIP_FAR)
    held["t", 3] = swap(after(held["t", 2], held["far tabs"], *sent), FLIP_NEAR)
    held.fence()
    sent = pick_rows(2)
    held["g", 3] = after(last_g, *sent)
    send_full(3)
    run_expert(1)
    held.fence()
    send_rows(1)
    pick_rows(3)
    run_expert(2)
    held.fence()
    send_rows(2)
    run_expert(3)
    held.fence()
    send_rows(3)
    held["part 2"] = sum_there(2)
    sums = jnp.stack([held["sums", c] for c in range(CHUNKS)])
    sums = sums.reshape(CHUNKS, 2, 2, many, tok_count)
    held["sums"] = sums[:, 0], swap(sums[:, 1], FLIP_X)
    held.fence()
    send_parts(3, *sum_there(3))
    sums = jnp.stack(held["sums"])
    held["sums"] = sums[:, :, 0], swap(sums[:, :, 1], FLIP_Y)
    held.fence()
    total = sum_here(3)
    held["part 2"] = [after(part, total) for part in held["part 2"]]
    send_parts(2, *held["part 2"])
    last = swap(total, FLIP_NEAR)
    send_parts(1, *sum_there(1))
    held["weight sums"] = sum_weights("g", ["act"], True, 2)
    held["sum 2"] = sum_here(2, [last], True)
    held.fence()
    held["far t"] = swap(held["sum 2"][0], FLIP_FAR)
    total_t, held["sum 1"] = sum_here(1, [], True)
    held["near t"] = swap(total_t, FLIP_NEAR)
    for name in (("out sent", 0), ("back sent", 0)):
        held[name] = after(held[name], total_t)
    send_rows(0)
    held["part 0"] = sum_there(0)
    held["weight sums"] = sum_weights("t", ["dgate", "dup"], False, 0, held["weight sums"])
    sums = jnp.stack(held["sums"])
    beyond = swap(after(sums[:, :, 2:], held["out got", 0], held["back got", 0]), FLIP_FAR)
    held["sums"] = sums[:, :, :2], beyond
    held.fence()

    def last_sum(name, flip, which):
        rows = (held[name + k, 0] for k in (" own", " got"))
        others = held[name + " part", 0], held["near " + which], held["far " + which]
        return token_sum(me, flip, capacity, table_of(0, 0), *rows, 0, others)

    held["far g"] = swap(held["sum 2"][1], FLIP_FAR)
    held["near g"] = swap(held["sum 1"], FLIP_NEAR)
    send_parts(0, *held["part 0"])
    weights_got = swap_dp(held["weight sums"][1])
    weight_grads = held["weight sums"][0] + weights_got.astype(F32)
    held["weight grads"] = weight_grads.astype(BF16)[None]
    held["total t"] = last_sum("out", FLIP_X, "t")
    sums = jnp.stack(held["sums"])
    beside = swap(after(sums[:, :, :, 1], held["total t"]), FLIP_NEAR)
    held["sums"] = sums[:, :, :, 0], beside
    held.fence()
    total_t, total_g = held["total t"], last_sum("back", FLIP_Y, "g")
    sums = jnp.stack(held["sums"], axis=1).reshape(CHUNKS, 2, 2, many, tok_count)
    parts = [sums[:, :, :, 0]] + [swap(sums[:, :, :, r], 4 * r) for r in range(1, many)]
    sums = jnp.stack(parts, axis=1).reshape(n_expert, tok_count)
    source = jnp.arange(n_expert, dtype=jnp.int32) ^ index
    hit = (expert_ids[:, :, None] == source[None, None, :]) & (slots >= 0)[:, :, None]
    gate_grads = jnp.sum(jnp.where(hit, sums.T[:, None, :], 0.0), axis=2)

    def scattered(total):
        if many == 1:
            return total
        parts = [total[r * tok_count : (r + 1) * tok_count] for r in range(many)]
        result = parts[0].astype(F32)
        for r in range(1, many):
            result = result + swap(parts[r], 4 * r).astype(F32)
        return result.astype(BF16)

    return (
        scattered(total_t),
        gate_grads,
        scattered(total_g),
        held["weight grads"],
    )


def solution(mesh):
    placed = (
        P(("dp", "expert"), None),
        P(("dp", "expert"), None),
        P(("dp", "expert"), None),
        P(("dp", "expert"), None),
        P(("dp", "expert"), None),
        P("expert", None, None, "dp"),
    )
    return jax.shard_map(
        local,
        mesh=mesh,
        in_specs=placed,
        out_specs=(
            P(("dp", "expert"), None),
            P(("dp", "expert"), None),
            P(("dp", "expert"), None),
            P("expert", None, None, "dp"),
        ),
        check_vma=False,
    )
```
